32 devices in a mesh: section: 4 (over x, core), expert: 8 (over z, y).
Axes of the slice: x: 2, y: 2, z: 4, core: 2. Of those that a mesh axis runs over, the one named last changes fastest.
Arguments:
- activations: bfloat16 [2, 2048, 5120], P(None, ('section', 'expert')), may hold values from -20 to 20
- norm_gain: float32 [5120], replicated, may hold values from 0.1 to 1.9
- router_weight: bfloat16 [5120, 32], P(None, ('section', 'expert')), may hold values from -0.078125 to 0.078125
- gate_proj: bfloat16 [4, 8, 768, 5120], P(None, 'expert', 'section'), may hold values from -0.078125 to 0.078125
- up_proj: bfloat16 [4, 8, 768, 5120], P(None, 'expert', 'section'), may hold values from -0.078125 to 0.078125
- down_proj: bfloat16 [4, 8, 768, 5120], P(None, 'expert', 'section'), may hold values from -0.21875 to 0.21875
- expert_ids: int32 [2, 2048, 2], P(None, ('section', 'expert')), may hold values from 0 to 31, all different within a row; in each aligned block of 64 rows (0 to 63, 64 to 127, ..., all dimensions but the last counted through in order) at most 8 rows name the same one
Outputs:
- mixture: bfloat16 [2, 2048, 5120], P(None, ('section', 'expert'))
The draws below stay inside these ranges and needn't reach their ends.
Inputs may be any that keep to these rules, and one draw needn't show every extreme that they name: `expert_ids`: in the rows of one device at one step (aligned blocks of 64 sequences), no expert is named more than 8 times, a bound that some block reaches; each row names 2 different experts.
All inputs are finite; a program needn't handle non-finite values.
Results may differ from the reference program's by a relative error of at most 0.0074.
Values may be sent and summed in bfloat16 or wider, within the bound.
No kernel may reach another device: no remote copies, remote signals or barrier semaphores. Data moves between devices by JAX's collectives and lax.ppermute only.
A program may use at most 192 MiB of HBM per device.

```python
import math
import jax
import jax.numpy as jnp
import numpy as np
from jax import lax

D = 5120
HID = 768
TOP = 2
STEPS = 2
SEQ_DEV = 64
EXPERTS = 32
SEQS = 2048
MOST = 8
N_SECTION = 4
N_EXPERT = 8


def draw_activations(key, part):
    key_values, key_columns = jax.random.split(key, 2)
    values = jnp.clip(jax.random.normal(key_values, (STEPS, SEQS, D), jnp.float32), -4.0, 4.0)
    columns = jnp.exp(jax.random.uniform(key_columns, (D,), jnp.float32, math.log(0.3), math.log(3.0)))
    return (values * columns).astype(jnp.bfloat16)


def level_of(own_key, dims, shards, least, top_value):
    level, own = 1.0, jax.random.fold_in(own_key, 6)
    for position, shards_of in shards:
        draws = jnp.exp(jax.random.uniform(jax.random.fold_in(own, position), (shards_of,), jnp.float32, least / len(shards), top_value / len(shards)))
        level = level * jnp.repeat(draws, dims[position] // shards_of).reshape([-1 if axis == position else 1 for axis in range(len(dims))])
    return level


def deal_out(stream_key, own, number, rows, count, top, most, lean):
    order = jax.random.permutation(stream_key, count)
    heavy_load, usual = portions_of(count, rows * top, most, lean, True), portions_of(count, rows * top, most, lean, False)
    places = jnp.arange(count)

    def named(lengths, rotation):
        used = int((lengths > 0).sum())
        fixed = max(1, used // 4)
        moved = fixed + (places - fixed + rotation * (used - fixed)) % max(1, count - fixed)
        return jnp.zeros((count,), jnp.int32).at[order[jnp.where(places < fixed, places, moved)]].set(jnp.asarray(lengths, jnp.int32))

    lengths = jnp.where(number % 4 == 0, named(heavy_load, number // 4), named(usual, number - number // 4 - 1))
    mixed = jax.random.permutation(jax.random.fold_in(own, 3), count)
    giver, taker = mixed[0:count // 2 * 2:2], mixed[1:count // 2 * 2:2]
    slack = jnp.minimum(lengths[giver] - 1, most - lengths[taker]) // 2
    slack = jnp.where((giver == order[0]) | (taker == order[0]) | (lengths[taker] == 0), 0, jnp.maximum(slack, 0))
    moved = jax.random.randint(jax.random.fold_in(own, 4), (count // 2,), 0, 1 << 20) % (slack + 1)
    lengths = lengths.at[giver].add(-moved).at[taker].add(moved)
    labels = jnp.searchsorted(jnp.cumsum(lengths), jnp.arange(rows * top), side="right").astype(jnp.int32)
    listing = labels.reshape(top, rows).T
    listing = listing[jax.random.permutation(jax.random.fold_in(own, 1), rows)]
    rotation = jax.random.randint(jax.random.fold_in(own, 2), (rows, 1), 0, top)
    return jnp.take_along_axis(listing, (jnp.arange(top)[None, :] + rotation) % top, axis=1)


def portions_of(number_of, total, reach, lean, full):
    portions = [(1 << 20) // math.isqrt(standing ** lean) + 1 for standing in range(1, number_of + 1)]
    largest = reach if full else min(reach, max(-(-total // number_of), total * portions[0] // sum(portions)))
    least = 1 if total - largest >= number_of - 1 else 0
    holding, spare = [largest] + [least] * (number_of - 1), total - largest - least * (number_of - 1)
    while spare > 0:
        free = [i for i in range(1, number_of) if holding[i] < largest] or [i for i in range(1, number_of) if holding[i] < reach]
        whole, budget = sum([portions[i] for i in free]), spare
        for i in free:
            more = min(reach - holding[i], max(1, budget * portions[i] // whole), spare)
            holding[i] = holding[i] + more
            spare = spare - more
    return np.array(holding)


def scatter_about(stream_key, dims, width, reach, cuts=(), kind=jnp.bfloat16):
    gain = level_of(stream_key, dims, cuts, -0.22, 0.18) if cuts else 1.0
    values = jax.random.normal(stream_key, dims, jnp.float32) * width * gain
    return jnp.minimum(jnp.maximum(values, -reach), reach).astype(kind)


def setup_inputs(seed: int = 0) -> dict:
    splits = jax.random.split(jax.random.key(seed), 8)
    activations = draw_activations(jax.random.fold_in(splits[7], 71), 0)
    norm_gain = jnp.clip(1.0 + 0.18 * jax.random.normal(splits[1], (D,), jnp.float32), 0.1, 1.9)
    router_weight = scatter_about(splits[2], (D, EXPERTS), D ** -0.5, 0.078125, ((1, 32),))
    gate_proj = scatter_about(splits[3], (N_SECTION, N_EXPERT, HID, D), D ** -0.5, 0.078125, ((1, 8), (2, 4)))
    up_proj = scatter_about(splits[4], (N_SECTION, N_EXPERT, HID, D), D ** -0.5, 0.078125, ((1, 8), (2, 4)))
    down_proj = scatter_about(splits[5], (N_SECTION, N_EXPERT, HID, D), HID ** -0.5, 0.21875, ((1, 8), (2, 4)))
    expert_ids_keys = jax.random.split(jax.random.fold_in(splits[6], 1), STEPS * SEQS // SEQ_DEV)
    expert_ids_turns = jax.random.permutation(jax.random.fold_in(splits[6], 3), STEPS * SEQS // SEQ_DEV)
    expert_ids = jax.vmap(lambda own, number: deal_out(jax.random.fold_in(splits[6], 2), own, number, SEQ_DEV, EXPERTS, TOP, MOST, 2))(expert_ids_keys, expert_ids_turns).reshape((STEPS, SEQS, TOP))
    return {"activations": activations, "norm_gain": norm_gain, "router_weight": router_weight, "gate_proj": gate_proj, "up_proj": up_proj, "down_proj": down_proj, "expert_ids": expert_ids}


epsilon = 1e-05
group_rows = 64
contract = (((1,), (1,)), ((), ()))

def expert_apply(inputs, gate_matrix, up_matrix, down_matrix, router_row):
    gate_part = lax.dot_general(inputs, gate_matrix, contract, preferred_element_type=jnp.float32)
    up_part = lax.dot_general(inputs, up_matrix, contract, preferred_element_type=jnp.float32)
    hidden = (jax.nn.silu(gate_part) * up_part).astype(jnp.bfloat16)
    result = jnp.dot(hidden, down_matrix, preferred_element_type=jnp.float32)
    logits = jnp.dot(inputs, router_row, preferred_element_type=jnp.float32)
    return (result.astype(jnp.bfloat16), jax.nn.sigmoid(logits).astype(jnp.bfloat16))

def reference(activations, norm_gain, router_weight, gate_proj, up_proj, down_proj, expert_ids):
    experts = N_SECTION * N_EXPERT
    gate_all = gate_proj.reshape(experts, HID, D)
    up_all = up_proj.reshape(experts, HID, D)
    down_all = down_proj.reshape(experts, HID, D)
    router_rows = router_weight.T
    outputs = []
    for step_index in range(STEPS):
        current = activations[step_index].astype(jnp.float32)
        inverse_rms = lax.rsqrt(lax.optimization_barrier(jnp.mean(current * current, axis=1, keepdims=True)) + epsilon)
        normed = (current * inverse_rms * norm_gain).astype(jnp.bfloat16)
        chosen = expert_ids[step_index].reshape(-1).astype(jnp.int32)
        pick_count = chosen.shape[0]
        sort_order = jnp.argsort(chosen, stable=True).astype(jnp.int32)
        sorted_rows = jnp.repeat(normed, TOP, axis=0)[sort_order]
        padded_rows = jnp.concatenate([sorted_rows, jnp.zeros((group_rows, D), sorted_rows.dtype)], axis=0)
        counts = lax.optimization_barrier(jnp.sum((chosen[:, None] == jnp.arange(experts, dtype=jnp.int32)[None, :]).astype(jnp.int32), axis=0))
        starts = (jnp.cumsum(counts) - counts).astype(jnp.int32)
        out_init = jnp.zeros((pick_count + group_rows, D), jnp.bfloat16)
        score_init = jnp.zeros((pick_count + group_rows,), jnp.bfloat16)

        def per_expert(buffers, pieces):
            gate_one, up_one, down_one, router_row, first_row, row_count = pieces

            def one_group(group_index, inner_buffers):
                out_buffer, score_buffer = inner_buffers
                row_start = (first_row + group_index * group_rows).astype(jnp.int32)
                group_input = lax.dynamic_slice_in_dim(padded_rows, row_start, group_rows, 0)
                result, gate_score = expert_apply(group_input, gate_one, up_one, down_one, router_row)
                out_buffer = lax.dynamic_update_slice_in_dim(out_buffer, result, row_start, 0)
                score_buffer = lax.dynamic_update_slice_in_dim(score_buffer, gate_score, row_start, 0)
                return (out_buffer, score_buffer)
            groups = (row_count + group_rows - 1) // group_rows
            return (lax.fori_loop(0, groups, one_group, buffers), None)
        (out_buffer, score_buffer), unused = lax.scan(per_expert, (out_init, score_init), (gate_all, up_all, down_all, router_rows, starts, counts))
        inverse = jnp.zeros((pick_count,), jnp.int32).at[sort_order].set(jnp.arange(pick_count, dtype=jnp.int32))
        picked = out_buffer[:pick_count][inverse].astype(jnp.float32).reshape(SEQS, TOP, D)
        weights = score_buffer[:pick_count][inverse].astype(jnp.float32).reshape(SEQS, TOP)
        mixture_rows = lax.optimization_barrier(jnp.sum(picked * weights[:, :, None], axis=1)) / lax.optimization_barrier(jnp.sum(weights, axis=1, keepdims=True))
        outputs.append(mixture_rows.astype(jnp.bfloat16))
    return jnp.stack(outputs)
```

```python
import jax
import jax.numpy as jnp
from jax import lax
from jax.sharding import Mesh, PartitionSpec as P

epsilon = 1e-05
contract = (((1,), (1,)), ((), ()))
swap = [(0, 1), (1, 0)]
group = ("core", "expert")


def side_swap(values):
    return lax.ppermute(values, "side", swap)


def core_swap(values):
    return lax.ppermute(values, "core", swap)


def cross_swap(values):
    return lax.ppermute(values, ("side", "core"), [(0, 3), (1, 2), (2, 1), (3, 0)])


def normalise(rows, norm_gain):
    current = rows.astype(jnp.float32)
    inverse_rms = lax.rsqrt(jnp.mean(current * current, axis=1, keepdims=True) + epsilon)
    return (current * inverse_rms * norm_gain).astype(jnp.bfloat16)


def on_device(activations, norm_gain, router_weight, gate_proj, up_proj, down_proj, expert_ids):
    steps, rows, width = activations.shape
    top = expert_ids.shape[2]
    columns = lax.axis_size("expert")
    cores = lax.axis_size("core")
    local = gate_proj.shape[0] // cores
    experts = gate_proj.shape[0] * columns
    capacity = max(2, 2 * top * rows // experts)
    part = gate_proj.shape[2]
    half = width // 2
    side = lax.axis_index("side")
    core = lax.axis_index("core")
    peers = cores * columns

    pack, member = [], []
    for step in range(steps):
        named = jnp.any(
            expert_ids[step][:, :, None] == jnp.arange(experts, dtype=jnp.int32), axis=1
        )
        count = named.astype(jnp.int32)
        earlier = jnp.cumsum(count, axis=0) - count
        taken = named[:, :, None] & (earlier[:, :, None] == jnp.arange(capacity, dtype=jnp.int32))
        taken = taken.reshape(rows, cores, local, columns, capacity)
        pack.append(
            [
                taken[:, :, i].reshape(rows, peers * capacity).T.astype(jnp.bfloat16)
                for i in range(local)
            ]
        )
        member.append(named)

    normed = [normalise(activations[step], norm_gain) for step in range(steps)]

    router_rows = lax.all_gather(
        router_weight.reshape(1, width), ("side", "core", "expert"), axis=0, tiled=True
    )

    gate_up, down_near, down_far = [], [], []
    for i in range(local):
        mine, theirs = core * local + i, (1 - core) * local + i

        def expert_of(weights, index):
            return lax.dynamic_index_in_dim(weights, index, 0, keepdims=False)[0]

        def down_block(index, which):
            return lax.dynamic_slice(
                down_proj, (index, 0, 0, which * half), (1, 1, part, half)
            ).reshape(part, half)

        gate_up.append(
            jnp.concatenate(
                [
                    expert_of(gate_proj, mine),
                    core_swap(expert_of(gate_proj, theirs)),
                    expert_of(up_proj, mine),
                    core_swap(expert_of(up_proj, theirs)),
                ],
                axis=0,
            )
        )
        down_near.append(
            jnp.concatenate([down_block(mine, side), core_swap(down_block(theirs, side))], axis=0)
        )
        down_far.append(
            jnp.concatenate(
                [
                    side_swap(down_block(mine, 1 - side)),
                    cross_swap(down_block(theirs, 1 - side)),
                ],
                axis=0,
            )
        )

    scatter, total = [], []
    for step in range(steps):
        logits = lax.dot_general(
            normed[step], router_rows, contract, preferred_element_type=jnp.float32
        )
        score = jnp.where(member[step], jax.nn.sigmoid(logits).astype(jnp.bfloat16), 0)
        by_slot = score.reshape(rows, cores, local, columns)
        own = jnp.stack(
            [
                pack[step][i].T.reshape(rows, peers, capacity)
                * by_slot[:, :, i].reshape(rows, peers, 1)
                for i in range(local)
            ]
        )
        other = side_swap(own)
        zeros = jnp.zeros_like(own)
        both = jnp.concatenate(
            [jnp.stack([own, zeros], axis=3), jnp.stack([zeros, other], axis=3)], axis=1
        )
        scatter.append(both.reshape(local, 2 * rows, peers * 2 * capacity))
        total.append(
            jnp.sum(both.astype(jnp.float32), axis=(0, 2, 3, 4)).reshape(2 * rows, 1)
        )

    numerators = [0.0] * steps
    for i in range(local):
        for step in range(steps):
            outgoing = jnp.dot(pack[step][i], normed[step]).reshape(peers, capacity, width)
            near = lax.all_to_all(outgoing, group, split_axis=0, concat_axis=0, tiled=True)
            far = side_swap(near)
            inputs = jnp.stack([near, far], axis=1).reshape(-1, width)
            products = lax.dot_general(
                inputs, gate_up[i], contract, preferred_element_type=jnp.float32
            )
            gate_part, up_part = jnp.split(products, 2, axis=1)
            hidden = (jax.nn.silu(gate_part) * up_part).astype(jnp.bfloat16)
            units = hidden.shape[1]
            other_hidden = side_swap(
                jnp.flip(hidden.reshape(peers, 2, capacity, units), axis=1).reshape(-1, units)
            )
            result = jnp.dot(
                jnp.concatenate([hidden, other_hidden], axis=1),
                jnp.concatenate([down_near[i], down_far[i]], axis=0),
                preferred_element_type=jnp.float32,
            ).astype(jnp.bfloat16)
            returned = lax.all_to_all(
                result.reshape(peers, 2 * capacity, half),
                group,
                split_axis=0,
                concat_axis=0,
                tiled=True,
            ).reshape(-1, half)
            numerators[step] += jnp.dot(
                scatter[step][i], returned, preferred_element_type=jnp.float32
            )

    outputs = []
    for step in range(steps):
        mixture = (numerators[step] / total[step]).astype(jnp.bfloat16)
        own, received = mixture[:rows], side_swap(mixture[rows:])
        low = jnp.where(side == 0, own, received)
        high = jnp.where(side == 0, received, own)
        outputs.append(jnp.concatenate([low, high], axis=1))
    return jnp.stack(outputs)


def solution(mesh):
    sections, columns = mesh.shape["section"], mesh.shape["expert"]
    split = Mesh(mesh.devices.reshape(2, sections // 2, columns), ("side", "core", "expert"))
    everywhere = ("side", "core", "expert")
    weights = P(None, "expert", ("side", "core"), None)
    return jax.shard_map(
        on_device,
        mesh=split,
        in_specs=(
            P(None, everywhere, None),
            P(),
            P(None, everywhere),
            weights,
            weights,
            weights,
            P(None, everywhere, None),
        ),
        out_specs=P(None, everywhere, None),
        check_vma=False,
    )
```

```python
import jax
import jax.numpy as jnp
from jax import lax
from jax.sharding import Mesh, PartitionSpec as P

epsilon = 1e-05
contract = (((1,), (1,)), ((), ()))
swap = [(0, 1), (1, 0)]
group = ("core", "inner")


def side_swap(values):
    return lax.ppermute(values, "side", swap)


def core_swap(values):
    return lax.ppermute(values, "core", swap)


def far_swap(values):
    return lax.ppermute(values, "far", swap)


def cross_swap(values):
    return lax.ppermute(values, ("side", "core"), [(0, 3), (1, 2), (2, 1), (3, 0)])


def normalise(rows, norm_gain):
    current = rows.astype(jnp.float32)
    inverse_rms = lax.rsqrt(jnp.mean(current * current, axis=-1, keepdims=True) + epsilon)
    return (current * inverse_rms * norm_gain).astype(jnp.bfloat16)


def all_router_rows(router_weight):
    axes = ("side", "core", "far", "inner")
    row = router_weight.reshape(1, -1)
    copies = jnp.broadcast_to(row, (lax.axis_size(axes), row.shape[1]))
    return lax.all_to_all(copies, axes, split_axis=0, concat_axis=0, tiled=True)


def on_device(activations, norm_gain, router_weight, gate_proj, up_proj, down_proj, expert_ids):
    steps, rows, width = activations.shape
    top = expert_ids.shape[2]
    cores, fars, inners = (lax.axis_size(name) for name in ("core", "far", "inner"))
    local = gate_proj.shape[0] // cores
    experts = gate_proj.shape[0] * fars * inners
    capacity = max(2, 2 * top * rows // experts)
    part = gate_proj.shape[2]
    half = width // 2
    side, core, far = (lax.axis_index(name) for name in ("side", "core", "far"))
    peers = cores * inners
    slots = local * capacity

    raw = [[activations[step], far_swap(activations[step])] for step in range(steps)]
    crossed = [step % 2 == 1 for step in range(steps)]
    raw_other = [
        [side_swap(raw[step][kind]) for kind in range(2)] if crossed[step] else None
        for step in range(steps)
    ]

    ids = jnp.stack([expert_ids, side_swap(expert_ids)])
    ids = jnp.stack([ids, far_swap(ids)])
    named = jnp.any(ids[..., None] == jnp.arange(experts, dtype=jnp.int32), axis=4)
    lower = jnp.tril(jnp.ones((rows, rows), jnp.bfloat16), -1)
    earlier = jnp.einsum(
        "rq,kpsqe->kpsre", lower, named.astype(jnp.bfloat16), preferred_element_type=jnp.float32
    )
    near_half = (2, 2, steps, rows, cores, local, fars, inners)
    mine = lax.dynamic_index_in_dim(named.reshape(near_half), far, 6, keepdims=False)
    rank = lax.dynamic_index_in_dim(earlier.reshape(near_half), far, 6, keepdims=False)
    taken = mine[..., None] & (rank[..., None] == jnp.arange(capacity, dtype=jnp.float32))
    taken = jnp.moveaxis(taken, 5, 6).astype(jnp.bfloat16)

    def expert_block(weights, which_core):
        return lax.dynamic_slice_in_dim(weights, which_core * local, local, 0)[:, 0]

    def down_block(which_core, which_side):
        return lax.dynamic_slice(
            down_proj,
            (which_core * local, 0, 0, which_side * half),
            (local, 1, part, half),
        )[:, 0]

    down_side = side_swap(down_block(core, 1 - side))
    down_cross = cross_swap(down_block(1 - core, 1 - side))
    gate_up = jnp.concatenate(
        [
            expert_block(gate_proj, core),
            core_swap(expert_block(gate_proj, 1 - core)),
            expert_block(up_proj, core),
            core_swap(expert_block(up_proj, 1 - core)),
        ],
        axis=1,
    )
    down = jnp.concatenate(
        [
            down_block(core, side),
            core_swap(down_block(1 - core, side)),
            down_side,
            down_cross,
        ],
        axis=1,
    )
    gate_up, down = lax.optimization_barrier((gate_up, down))

    router_rows = all_router_rows(router_weight)
    normed = [normalise(activations[step], norm_gain) for step in range(steps)]
    own_named = named[0, 0]
    scores = []
    for step in range(steps):
        logits = lax.dot_general(
            normed[step], router_rows, contract, preferred_element_type=jnp.float32
        )
        scores.append(
            jnp.where(own_named[step], jax.nn.sigmoid(logits).astype(jnp.bfloat16), 0)
        )
    scores = jnp.stack(scores)
    scores = jnp.stack([scores, side_swap(scores)])
    total = jnp.sum(scores.astype(jnp.float32), axis=3, keepdims=True)
    scores = jnp.stack([scores, far_swap(scores)])
    near_scores = lax.dynamic_index_in_dim(scores.reshape(near_half), far, 6, keepdims=False)
    weighted = taken * jnp.moveaxis(near_scores, 5, 6)[..., None]
    planes = jnp.eye(2, dtype=jnp.bfloat16)
    scatter = jnp.einsum("kpsrcnlt,pq->ksprcnqlt", weighted, planes).reshape(
        2, steps, 2 * rows, peers * 2 * slots
    )

    def forward(step, kind):
        if crossed[step]:
            source = jnp.concatenate([raw[step][kind], raw_other[step][kind]], axis=0)
            pack = jnp.einsum("prcnlt,pq->cnqltpr", taken[kind, :, step], planes)
            pack = pack.reshape(peers * 2 * slots, 2 * rows)
            outgoing = jnp.dot(pack, normalise(source, norm_gain)).reshape(
                peers, 2 * slots, width
            )
            both = lax.all_to_all(outgoing, group, split_axis=0, concat_axis=0, tiled=True)
            both = both.reshape(peers, 2, local, capacity, width)
        else:
            pack = jnp.einsum("rcnlt->cnltr", taken[kind, 0, step]).reshape(peers * slots, rows)
            outgoing = jnp.dot(pack, normalise(raw[step][kind], norm_gain)).reshape(
                peers, slots, width
            )
            near = lax.all_to_all(outgoing, group, split_axis=0, concat_axis=0, tiled=True)
            other = side_swap(near)
            both = jnp.stack([near, other], axis=1).reshape(peers, 2, local, capacity, width)
        return both

    def apply(both):
        inputs = jnp.moveaxis(both, 2, 0).reshape(local, -1, width)
        products = jnp.einsum("ird,iud->iru", inputs, gate_up, preferred_element_type=jnp.float32)
        gate_part, up_part = jnp.split(products, 2, axis=2)
        hidden = (jax.nn.silu(gate_part) * up_part).astype(jnp.bfloat16)
        units = hidden.shape[2]
        flipped = jnp.flip(hidden.reshape(local, peers, 2, capacity, units), axis=2)
        other_hidden = side_swap(flipped.reshape(hidden.shape))
        result = jnp.einsum(
            "iru,iud->ird",
            jnp.concatenate([hidden, other_hidden], axis=2),
            down,
            preferred_element_type=jnp.float32,
        ).astype(jnp.bfloat16)
        result = jnp.moveaxis(result.reshape(local, peers, 2, capacity, half), 0, 2)
        returned = lax.all_to_all(
            result.reshape(peers, 2 * slots, half),
            group,
            split_axis=0,
            concat_axis=0,
            tiled=True,
        )
        return returned.reshape(-1, half)

    outputs = []
    for step in range(steps):
        sums = [
            jnp.dot(
                scatter[kind, step],
                apply(forward(step, kind)),
                preferred_element_type=jnp.float32,
            )
            for kind in (0, 1)
        ]
        from_far = far_swap(sums[1].astype(jnp.bfloat16)).astype(jnp.float32)
        mixture = (sums[0] + from_far) / total[:, step].reshape(2 * rows, 1)
        mixture = mixture.astype(jnp.bfloat16)
        own, received = mixture[:rows], side_swap(mixture[rows:])
        low = jnp.where(side == 0, own, received)
        high = jnp.where(side == 0, received, own)
        outputs.append(jnp.concatenate([low, high], axis=1))
    return jnp.stack(outputs)


def solution(mesh):
    sections, columns = mesh.shape["section"], mesh.shape["expert"]
    split = Mesh(
        mesh.devices.reshape(2, sections // 2, 2, columns // 2),
        ("side", "core", "far", "inner"),
    )
    everywhere = ("side", "core", "far", "inner")
    weights = P(None, ("far", "inner"), ("side", "core"), None)
    return jax.shard_map(
        on_device,
        mesh=split,
        in_specs=(
            P(None, everywhere, None),
            P(),
            P(None, everywhere),
            weights,
            weights,
            weights,
            P(None, everywhere, None),
        ),
        out_specs=P(None, everywhere, None),
        check_vma=False,
    )
```

```python
import jax
import jax.numpy as jnp
from jax import lax
from jax.experimental import pallas as pl
from jax.experimental.pallas import tpu as pltpu
from jax.sharding import Mesh, PartitionSpec as P

epsilon = 1e-05
contract = (((1,), (1,)), ((), ()))
swap = [(0, 1), (1, 0)]
group = ("core", "inner")
everywhere = ("side", "core", "far", "inner")
vmem_bytes = 48 * 2**20
lanes = 128


def side_swap(values):
    return lax.ppermute(values, "side", swap)


def core_swap(values):
    return lax.ppermute(values, "core", swap)


def far_swap(values):
    return lax.ppermute(values, "far", swap)


def cross_swap(values):
    return lax.ppermute(values, ("side", "core"), [(0, 3), (1, 2), (2, 1), (3, 0)])


def send(values):
    return lax.all_to_all(values, group, split_axis=0, concat_axis=0, tiled=True)


def tie(*values):
    return lax.optimization_barrier(values)


def normalise(rows, norm_gain):
    current = rows.astype(jnp.float32)
    inverse_rms = lax.rsqrt(jnp.mean(current * current, axis=-1, keepdims=True) + epsilon)
    return (current * inverse_rms * norm_gain).astype(jnp.bfloat16)


def hidden_kernel(place, inputs, router, gate_own, up_own, gate_got, up_got, hidden, score):
    def work(gate, up):
        rows = inputs[0]
        gate_part = lax.dot_general(rows, gate, contract, preferred_element_type=jnp.float32)
        up_part = lax.dot_general(rows, up, contract, preferred_element_type=jnp.float32)
        hidden[0, 0] = (gate_part / (1.0 + jnp.exp(-gate_part)) * up_part).astype(jnp.bfloat16)

    @pl.when(pl.program_id(1) == 0)
    def _():
        work(gate_own[0, 0], up_own[0, 0])
        logits = lax.dot_general(
            inputs[0], router[0], contract, preferred_element_type=jnp.float32
        )
        gated = (1.0 / (1.0 + jnp.exp(-logits[:, :1]))).astype(jnp.bfloat16)
        score[0] = jnp.broadcast_to(gated, score.shape[1:])

    @pl.when(pl.program_id(1) == 1)
    def _():
        work(gate_got[0], up_got[0])


def make_hidden(place, inputs, router, gate_proj, up_proj, gate_got, up_got):
    local, rows, width = inputs.shape
    part = gate_proj.shape[2]
    own = pl.BlockSpec((1, 1, part, width), lambda i, j, place: (place[0] * local + i, 0, 0, 0))
    got = pl.BlockSpec((1, part, width), lambda i, j, place: (i, 0, 0))
    return pl.pallas_call(
        hidden_kernel,
        grid_spec=pltpu.PrefetchScalarGridSpec(
            num_scalar_prefetch=1,
            grid=(local, 2),
            in_specs=[
                pl.BlockSpec((1, rows, width), lambda i, j, place: (i, 0, 0)),
                pl.BlockSpec((1, router.shape[1], width), lambda i, j, place: (i, 0, 0)),
                own,
                own,
                got,
                got,
            ],
            out_specs=[
                pl.BlockSpec((1, 1, rows, part), lambda i, j, place: (i, j, 0, 0)),
                pl.BlockSpec((1, rows, lanes), lambda i, j, place: (i, 0, 0)),
            ],
        ),
        out_shape=[
            jax.ShapeDtypeStruct((local, 2, rows, part), jnp.bfloat16),
            jax.ShapeDtypeStruct((local, rows, lanes), jnp.bfloat16),
        ],
        compiler_params=pltpu.CompilerParams(vmem_limit_bytes=vmem_bytes),
        cost_estimate=pl.CostEstimate(flops=1, bytes_accessed=1, transcendentals=0),
    )(place, inputs, router, gate_proj, up_proj, gate_got, up_got)


def result_kernel(
    place, hidden, other, score, down_own, down_core, down_side, down_cross, result
):
    middle = hidden.shape[2] // 2
    half = down_core.shape[2]

    def product(values, weights):
        return jnp.dot(values, weights, preferred_element_type=jnp.float32)

    low, high = pl.ds(0, middle), pl.ds(middle, middle)
    for here, there in ((low, high), (high, low)):
        total = product(hidden[0, 0, here, :], down_own[0, 0])
        total += product(hidden[0, 1, here, :], down_core[0])
        total += product(other[0, 0, there, :], down_side[0])
        total += product(other[0, 1, there, :], down_cross[0])
        gated = total * score[0, here, :1].astype(jnp.float32)
        result[0, here, :half] = gated.astype(jnp.bfloat16)
    result[0, :, half:] = score[0]


def make_result(place, hidden, other, score, down_proj, down_core, down_side, down_cross):
    local, parts, rows, part = hidden.shape
    half = down_core.shape[2]
    units = pl.BlockSpec((1, parts, rows, part), lambda i, place: (i, 0, 0, 0))
    got = pl.BlockSpec((1, part, half), lambda i, place: (i, 0, 0))
    return pl.pallas_call(
        result_kernel,
        grid_spec=pltpu.PrefetchScalarGridSpec(
            num_scalar_prefetch=1,
            grid=(local,),
            in_specs=[
                units,
                units,
                pl.BlockSpec((1, rows, lanes), lambda i, place: (i, 0, 0)),
                pl.BlockSpec(
                    (1, 1, part, half), lambda i, place: (place[0] * local + i, 0, 0, place[1])
                ),
                got,
                got,
                got,
            ],
            out_specs=pl.BlockSpec((1, rows, half + lanes), lambda i, place: (i, 0, 0)),
        ),
        out_shape=jax.ShapeDtypeStruct((local, rows, half + lanes), jnp.bfloat16),
        compiler_params=pltpu.CompilerParams(vmem_limit_bytes=vmem_bytes),
        cost_estimate=pl.CostEstimate(flops=1, bytes_accessed=1, transcendentals=0),
    )(place, hidden, other, score, down_proj, down_core, down_side, down_cross)


def on_device(activations, norm_gain, router_weight, gate_proj, up_proj, down_proj, expert_ids):
    steps, rows, width = activations.shape
    top = expert_ids.shape[2]
    cores, fars, inners = (lax.axis_size(name) for name in ("core", "far", "inner"))
    local = gate_proj.shape[0] // cores
    experts = gate_proj.shape[0] * fars * inners
    capacity = max(2, 2 * top * rows // experts)
    part = gate_proj.shape[2]
    half = width // 2
    side, core, far = (lax.axis_index(name) for name in ("side", "core", "far"))
    place = jnp.stack([core, side]).astype(jnp.int32)
    peers = cores * inners
    slots = local * capacity
    two = jnp.eye(2, dtype=jnp.bfloat16)
    near_half = (steps, rows, cores, local, fars, inners)
    lower = jnp.tril(jnp.ones((rows, rows), jnp.bfloat16), -1)

    def slots_of(ids):
        named = jnp.any(ids[..., None] == jnp.arange(experts, dtype=jnp.int32), axis=2)
        earlier = jnp.einsum(
            "rq,sqe->sre", lower, named.astype(jnp.bfloat16), preferred_element_type=jnp.float32
        )
        mine = lax.dynamic_index_in_dim(named.reshape(near_half), far, 4, keepdims=False)
        rank = lax.dynamic_index_in_dim(earlier.reshape(near_half), far, 4, keepdims=False)
        taken = mine[..., None] & (rank[..., None] == jnp.arange(capacity, dtype=jnp.float32))
        return jnp.moveaxis(taken, 3, 4).astype(jnp.bfloat16)

    def single(taken, source):
        pack = jnp.einsum("rcnlt->cnltr", taken).reshape(peers * slots, rows)
        return jnp.dot(pack, normalise(source, norm_gain)).reshape(peers, slots, width)

    def double(taken, source, other):
        pack = jnp.einsum("prcnlt,pq->cnqltpr", jnp.stack(taken), two)
        pack = pack.reshape(peers * 2 * slots, 2 * rows)
        stacked = jnp.concatenate([source, other], axis=0)
        return jnp.dot(pack, normalise(stacked, norm_gain)).reshape(peers, 2 * slots, width)

    def expert_block(weights, which_core):
        return lax.dynamic_slice_in_dim(weights, which_core * local, local, 0)[:, 0]

    def down_block(which_core, which_side, i=None):
        first, count = (0, local) if i is None else (i, 1)
        return lax.dynamic_slice(
            down_proj,
            (which_core * local + first, 0, 0, which_side * half),
            (count, 1, part, half),
        )[:, 0]

    first, second = activations[0], activations[1]

    own_taken = slots_of(expert_ids)
    side_ids = side_swap(expert_ids)
    first_side = side_swap(first)
    first_far = far_swap(first)
    second_own = send(single(own_taken[1], second))
    far_ids = far_swap(jnp.stack([expert_ids, side_ids]))
    side_blocks = down_block(core, 1 - side)
    down_side = [side_swap(side_blocks[:1])]
    side_taken = slots_of(side_ids)
    outgoing = double([own_taken[0], side_taken[0]], first, first_side)
    gate_send, up_send = expert_block(gate_proj, 1 - core), expert_block(up_proj, 1 - core)
    outgoing, second_own, first_far, far_ids, down_side[0], side_blocks, second, gate_send, up_send = tie(
        outgoing, second_own, first_far, far_ids, down_side[0], side_blocks, second, gate_send, up_send
    )

    first_own = send(outgoing)
    first_far_side = side_swap(first_far)
    second_far = far_swap(second)
    down_side.append(side_swap(side_blocks[1:]))
    gate_got, up_got = core_swap(gate_send), core_swap(up_send)
    far_taken = slots_of(far_ids[0])
    far_side_taken = slots_of(far_ids[1])
    outgoing = double([far_taken[0], far_side_taken[0]], first_far, first_far_side)
    cross_blocks = down_block(1 - core, 1 - side)
    column = router_weight.reshape(1, width)
    column_got = core_swap(column)
    pair = jnp.where(
        core == 0,
        jnp.concatenate([column, column_got]),
        jnp.concatenate([column_got, column]),
    )
    outgoing, first_own, second_far, down_side[1], gate_got, up_got, cross_blocks, pair = tie(
        outgoing, first_own, second_far, down_side[1], gate_got, up_got, cross_blocks, pair
    )

    first_relay = send(outgoing)
    second_far_side = side_swap(second_far)
    pair_got = side_swap(pair)
    router = jnp.where(side == core, pair, pair_got)
    router = jnp.broadcast_to(router[:, None], (local, 16, width))
    down_cross = [cross_swap(cross_blocks[:1])]
    outgoing = double([far_taken[1], far_side_taken[1]], second_far, second_far_side)
    core_blocks = down_block(1 - core, side)

    def start_experts(inputs):
        hidden, score = make_hidden(
            place, inputs.reshape(local, -1, width), router, gate_proj, up_proj, gate_got, up_got
        )
        return hidden, side_swap(hidden), score

    def finish_experts(hidden, other, score):
        result = make_result(
            place, hidden, other, score, down_proj, down_core, down_side, down_cross
        )
        result = result.reshape(local, 2, peers, capacity, half + lanes)
        return jnp.transpose(result, (2, 1, 0, 3, 4)).reshape(peers, 2 * slots, half + lanes)

    def mid(arrived):
        arrived = arrived.reshape(peers, 2, local, capacity, width)
        return jnp.transpose(arrived, (2, 1, 0, 3, 4))

    own_hidden = start_experts(mid(first_own))

    def adder(step, taken):
        taken = jnp.stack([each[step] for each in taken])
        return jnp.einsum("prcnlt,pq->prcnqlt", taken, two).reshape(
            2 * rows, peers * 2 * slots
        )

    own_adders = [adder(step, [own_taken, side_taken]) for step in range(steps)]
    far_adders = [adder(step, [far_taken, far_side_taken]) for step in range(steps)]
    outgoing, first_relay, down_cross[0], cross_blocks, core_blocks, own_hidden, router = tie(
        outgoing, first_relay, down_cross[0], cross_blocks, core_blocks, own_hidden, router
    )

    second_relay = send(outgoing)
    down_cross.append(cross_swap(cross_blocks[1:]))
    down_core = core_swap(core_blocks)
    down_side, down_cross = (jnp.concatenate(pieces, axis=0) for pieces in (down_side, down_cross))
    relay_hidden = start_experts(mid(first_relay))
    outgoing = jnp.concatenate(
        [finish_experts(*own_hidden), finish_experts(*relay_hidden)], axis=1
    )
    outgoing, second_relay, second_own, own_adders, far_adders = tie(
        outgoing, second_relay, second_own, own_adders, far_adders
    )

    first_back = send(outgoing)
    middle = peers // 2
    pieces = [side_swap(second_own[:middle])]
    relay_hidden = start_experts(mid(second_relay))
    relay_hidden, second_own = tie(relay_hidden, second_own)
    pieces.append(side_swap(second_own[middle:]))
    outgoing = finish_experts(*relay_hidden)
    outgoing, first_back, pieces[0] = tie(outgoing, first_back, pieces[0])

    def add(matrix, returned):
        return jnp.dot(
            matrix, returned.reshape(-1, half + lanes), preferred_element_type=jnp.float32
        )

    def to_far(sums):
        numerators, total = sums[:, :half].astype(jnp.bfloat16), sums[:, half:]
        whole = total.astype(jnp.bfloat16)
        rest = (total - whole.astype(jnp.float32)).astype(jnp.bfloat16)
        spot = jnp.arange(lanes) < lanes // 2
        return far_swap(jnp.concatenate([numerators, jnp.where(spot, whole, rest)], axis=1))

    def finish(near, received):
        received = received.astype(jnp.float32)
        total = near[:, half : half + 1] + received[:, half : half + 1] + received[:, -1:]
        mixture = ((near[:, :half] + received[:, :half]) / total).astype(jnp.bfloat16)
        return mixture[:rows], side_swap(mixture[rows:])

    def lay_out(own, received):
        low = jnp.where(side == 0, own, received)
        high = jnp.where(side == 0, received, own)
        return jnp.concatenate([low, high], axis=1)

    second_relay_back = send(outgoing)
    first_back = first_back.reshape(peers, 2, 2 * slots, half + lanes)
    first_received = to_far(add(far_adders[0], first_back[:, 1]))
    first_near = add(own_adders[0], first_back[:, 0])
    arrived = jnp.stack([second_own, jnp.concatenate(pieces, axis=0)])
    arrived = arrived.reshape(2, peers, local, capacity, width)
    outgoing = finish_experts(*start_experts(jnp.transpose(arrived, (2, 0, 1, 3, 4))))
    outgoing, second_relay_back, first_received, first_near = tie(
        outgoing, second_relay_back, first_received, first_near
    )

    second_own_back = send(outgoing)
    second_received = to_far(add(far_adders[1], second_relay_back))
    first_out = finish(first_near, first_received)
    second_own_back, first_out = tie(second_own_back, first_out)
    second_out = finish(add(own_adders[1], second_own_back), second_received)
    return jnp.stack([lay_out(*first_out), lay_out(*second_out)])


def solution(mesh):
    sections, columns = mesh.shape["section"], mesh.shape["expert"]
    split = Mesh(
        mesh.devices.reshape(2, sections // 2, 2, columns // 2),
        ("side", "core", "far", "inner"),
    )
    weights = P(None, ("far", "inner"), ("side", "core"), None)
    return jax.shard_map(
        on_device,
        mesh=split,
        in_specs=(
            P(None, everywhere, None),
            P(),
            P(None, everywhere),
            weights,
            weights,
            weights,
            P(None, everywhere, None),
        ),
        out_specs=P(None, everywhere, None),
        check_vma=False,
    )
```

```python
import functools

import jax
import jax.numpy as jnp
from jax import lax
from jax.experimental import pallas as pl
from jax.experimental.pallas import tpu as pltpu
from jax.sharding import Mesh, PartitionSpec as P

epsilon = 1e-05
contract = (((1,), (1,)), ((), ()))
swap = [(0, 1), (1, 0)]
group = ("core", "inner")
everywhere = ("side", "core", "far", "inner")
vmem_bytes = 48 * 2**20
lanes = 128
block_rows = 128


def side_swap(values):
    return lax.ppermute(values, "side", swap)


def core_swap(values):
    return lax.ppermute(values, "core", swap)


def far_swap(values):
    return lax.ppermute(values, "far", swap)


def cross_swap(values):
    return lax.ppermute(values, ("side", "core"), [(0, 3), (1, 2), (2, 1), (3, 0)])


def send(values):
    return lax.all_to_all(values, group, split_axis=0, concat_axis=0, tiled=True)


def tie(*values):
    return lax.optimization_barrier(values)


def normalise(rows, norm_gain):
    current = rows.astype(jnp.float32)
    inverse_rms = lax.rsqrt(jnp.mean(current * current, axis=-1, keepdims=True) + epsilon)
    return (current * inverse_rms * norm_gain).astype(jnp.bfloat16)


def cut_kernel(plan, place, *refs):
    sources, outputs = refs[:3], refs[3 : 3 + len(plan)]
    kept, (sems, out_sems) = refs[3 + len(plan) : -2], refs[-2:]
    copies = []
    for n, (chosen, other_core, first, other_side, offset) in enumerate(plan):
        columns = outputs[n].shape[2]
        count = outputs[n].shape[0] // len(chosen)
        core = 1 - place[0] if other_core else place[0]
        side = 1 - place[1] if other_side else place[1]
        for m, which in enumerate(chosen):
            source = sources[which]
            experts = pl.ds(core * (source.shape[0] // 2) + first, count)
            block = source.at[experts, 0]
            if columns < source.shape[3]:
                start = pl.multiple_of(side * (source.shape[3] // 2) + offset, lanes)
                block = source.at[experts, 0, :, pl.ds(start, columns)]
            spot = pl.ds(m * count, count)
            inner, outer = kept[n].at[spot], outputs[n].at[spot]
            copies.append(
                (
                    pltpu.make_async_copy(block, inner, sems.at[len(copies)]),
                    pltpu.make_async_copy(inner, outer, out_sems.at[len(copies)]),
                )
            )
    for inward, outward in copies:
        inward.start()
    for inward, outward in copies:
        inward.wait()
        outward.start()
    for inward, outward in copies:
        outward.wait()


def cut(place, weights, plan):
    anywhere = pl.BlockSpec(memory_space=pl.ANY)
    shapes = [jax.ShapeDtypeStruct(shape, jnp.bfloat16) for *_, shape in plan]
    total = sum(len(each[0]) for each in plan)
    return pl.pallas_call(
        functools.partial(cut_kernel, [each[:-1] for each in plan]),
        in_specs=[pl.BlockSpec(memory_space=pltpu.SMEM)] + [anywhere] * 3,
        out_specs=[anywhere] * len(plan),
        out_shape=shapes,
        scratch_shapes=[pltpu.VMEM(each.shape, each.dtype) for each in shapes]
        + [pltpu.SemaphoreType.DMA((total,))] * 2,
        compiler_params=pltpu.CompilerParams(vmem_limit_bytes=vmem_bytes),
        cost_estimate=pl.CostEstimate(flops=1, bytes_accessed=1, transcendentals=0),
    )(place, *weights)


def hidden_kernel(count, local, capacity, stride, place, *refs):
    inputs, (router, gate_proj, up_proj, got) = refs[:count], refs[count : count + 4]
    outputs, scratch = refs[count + 4 : -5], refs[-5:]
    hidden, score = outputs[:2]
    rows_kept, router_kept, weights, row_sems, weight_sems = scratch
    copies = [pltpu.make_async_copy(router, router_kept, row_sems.at[0])]
    first_row = 0
    for each in inputs:
        height = min(block_rows, each.shape[0])
        for start in range(0, each.shape[0], height):
            source, kept = each.at[pl.ds(start, height)], rows_kept.at[pl.ds(first_row, height)]
            copies.append(pltpu.make_async_copy(source, kept, row_sems.at[len(copies)]))
            first_row += height
    blocks = []
    for j in range(2):
        for i in range(local):
            if j == 0:
                sources = [ref.at[place[0] * local + i, 0] for ref in (gate_proj, up_proj)]
            else:
                sources = [got.at[i], got.at[local + i]]
            for n, source in enumerate(sources):
                blocks.append(
                    pltpu.make_async_copy(
                        source, weights.at[j, i, n], weight_sems.at[(j * local + i) * 2 + n]
                    )
                )
    for copy in copies + blocks[:2]:
        copy.start()
    for copy in copies:
        copy.wait()
    for copy in blocks[2:4]:
        copy.start()
    rows = rows_kept[...]
    owner = lax.broadcasted_iota(jnp.int32, (rows.shape[0], 1), 0) // capacity % local

    def product(matrix):
        return lax.dot_general(rows, matrix, contract, preferred_element_type=jnp.float32)

    gated = jnp.zeros((rows.shape[0], 1), jnp.float32)
    for i in range(local):
        logits = product(router_kept[i])
        gated = jnp.where(owner == i, 1.0 / (1.0 + jnp.exp(-logits[:, :1])), gated)
    score[...] = jnp.broadcast_to(gated, score.shape).astype(jnp.bfloat16)
    for j in range(2):
        chosen = None
        for i in range(local):
            for n in range(2):
                now = (j * local + i) * 2 + n
                blocks[now].wait()
                if now + 4 < len(blocks):
                    blocks[now + 4].start()
            gate_part = product(weights[j, i, 0])
            up_part = product(weights[j, i, 1])
            units = gate_part / (1.0 + jnp.exp(-gate_part)) * up_part
            chosen = units if i == 0 else jnp.where(owner == i, units, chosen)
        chosen = chosen.astype(jnp.bfloat16)
        hidden[j] = chosen
        for block in range(rows.shape[0] // stride if len(outputs) == 3 else 0):
            turned = pl.ds((block ^ 1) * stride, stride)
            outputs[2][j, turned, :] = chosen[block * stride : (block + 1) * stride]


def make_hidden(place, inputs, router, gate_proj, up_proj, got, capacity, stride):
    local, part, width = router.shape[0], *got.shape[1:]
    count = len(inputs)
    rows = sum(each.shape[0] for each in inputs)
    anywhere = pl.BlockSpec(memory_space=pl.ANY)
    near = pl.BlockSpec(memory_space=pltpu.VMEM)
    units = jax.ShapeDtypeStruct((2, rows, part), jnp.bfloat16)
    inside = stride % 16 == 0
    hidden, score, *flipped = pl.pallas_call(
        functools.partial(hidden_kernel, count, local, capacity, stride),
        in_specs=[pl.BlockSpec(memory_space=pltpu.SMEM)] + [anywhere] * (count + 4),
        out_specs=[near] * (3 if inside else 2),
        out_shape=[units, jax.ShapeDtypeStruct((rows, lanes), jnp.bfloat16)] + [units] * inside,
        scratch_shapes=[
            pltpu.VMEM((rows, width), jnp.bfloat16),
            pltpu.VMEM(router.shape, jnp.bfloat16),
            pltpu.VMEM((2, local, 2, part, width), jnp.bfloat16),
            pltpu.SemaphoreType.DMA((rows // min(16, rows) + 1,)),
            pltpu.SemaphoreType.DMA((4 * local,)),
        ],
        compiler_params=pltpu.CompilerParams(vmem_limit_bytes=vmem_bytes),
        cost_estimate=pl.CostEstimate(flops=1, bytes_accessed=1, transcendentals=0),
    )(place, *inputs, router, gate_proj, up_proj, got)
    if not inside:
        flipped = [jnp.flip(hidden.reshape(2, -1, 2, stride, part), axis=2).reshape(hidden.shape)]
    return hidden, score, flipped[0]


def result_kernel(local, capacity, place, hidden, other, score, down_proj, down_core, *refs):
    down_side, down_cross = refs[:local], refs[local : 3 * local]
    result, weights, sems = refs[3 * local :]
    part, half = down_core.shape[1:]
    blocks = []
    middle = half // 2
    for i in range(local):
        columns = pl.ds(pl.multiple_of(place[1] * half, lanes), half)
        kept = weights.at[i]
        pairs = [
            [(down_proj.at[place[0] * local + i, 0, :, columns], kept.at[0])],
            [(down_core.at[i], kept.at[1])],
            [(down_side[i].at[0], kept.at[2])],
            [
                (down_cross[2 * i].at[0], kept.at[3, :, pl.ds(0, middle)]),
                (down_cross[2 * i + 1].at[0], kept.at[3, :, pl.ds(middle, half - middle)]),
            ],
        ]
        for pair in pairs:
            blocks.append([])
            for source, spot in pair:
                sem = sems.at[sum(len(block) for block in blocks)]
                blocks[-1].append(pltpu.make_async_copy(source, spot, sem))
    for block in blocks:
        for copy in block:
            copy.start()
    rows = hidden.shape[1]
    owner = lax.broadcasted_iota(jnp.int32, (rows, 1), 0) // capacity % local
    units = [hidden[0], hidden[1], other[0], other[1]]
    total = None
    for i in range(local):
        for n in range(4):
            for copy in blocks[i * 4 + n]:
                copy.wait()
            mine = jnp.where(owner == i, units[n], jnp.zeros_like(units[n]))
            term = jnp.dot(mine, weights[i, n], preferred_element_type=jnp.float32)
            total = term if total is None else total + term
    gated = total * score[:, :1].astype(jnp.float32)
    result[:, :half] = gated.astype(jnp.bfloat16)
    result[:, half:] = score[...]


def make_result(place, hidden, other, score, down_proj, down_core, down_side, down_cross, capacity):
    local, part, half = down_core.shape
    rows = hidden.shape[1]
    anywhere = pl.BlockSpec(memory_space=pl.ANY)
    near = pl.BlockSpec(memory_space=pltpu.VMEM)
    return pl.pallas_call(
        functools.partial(result_kernel, local, capacity),
        in_specs=[pl.BlockSpec(memory_space=pltpu.SMEM)] + [near] * 3 + [anywhere] * (2 + 3 * local),
        out_specs=near,
        out_shape=jax.ShapeDtypeStruct((rows, half + lanes), jnp.bfloat16),
        scratch_shapes=[
            pltpu.VMEM((local, 4, part, half), jnp.bfloat16),
            pltpu.SemaphoreType.DMA((5 * local,)),
        ],
        compiler_params=pltpu.CompilerParams(vmem_limit_bytes=vmem_bytes),
        cost_estimate=pl.CostEstimate(flops=1, bytes_accessed=1, transcendentals=0),
    )(place, hidden, other, score, down_proj, down_core, *down_side, *down_cross)


def on_device(activations, norm_gain, router_weight, gate_proj, up_proj, down_proj, expert_ids):
    steps, rows, width = activations.shape
    top = expert_ids.shape[2]
    cores, fars, inners = (lax.axis_size(name) for name in ("core", "far", "inner"))
    local = gate_proj.shape[0] // cores
    experts = gate_proj.shape[0] * fars * inners
    capacity = max(2, 2 * top * rows // experts)
    part = gate_proj.shape[2]
    half = width // 2
    side, core, far = (lax.axis_index(name) for name in ("side", "core", "far"))
    place = jnp.stack([core, side]).astype(jnp.int32)
    peers = cores * inners
    slots = local * capacity
    places = experts * capacity

    def codes_of(ids):
        flat = ids.reshape(steps, 1, 1, -1)
        before = jnp.arange(rows * top, dtype=jnp.int32) // top < jnp.arange(
            rows, dtype=jnp.int32
        ).reshape(rows, 1, 1)
        earlier = jnp.sum(((ids[..., None] == flat) & before).astype(jnp.int32), axis=3)
        return ids * capacity + earlier

    def spots(kinds, kind, planes):
        shape = (cores, inners, kinds, planes, local, capacity)
        c, n, k, q, l, t = (lax.broadcasted_iota(jnp.int32, shape, axis) for axis in range(6))
        spot = ((((c * local + l) * fars + far) * inners + n) * capacity + t) + q * places
        return jnp.where(k == kind, spot, -1).reshape(-1)

    def both_planes(near, other):
        return jnp.concatenate([near, other + places], axis=0)

    def matching(left, right):
        return jnp.any(left == right, axis=0).astype(jnp.bfloat16)

    def spread(codes, planes):
        spot = spots(1, 0, planes)
        return matching(spot[None, :, None], codes.T[:, None, :])

    def gather(codes, kinds, kind):
        spot = spots(kinds, kind, 2)
        return matching(codes.T[:, :, None], spot[None, None, :])

    def single(codes, source):
        return jnp.dot(spread(codes, 1), normalise(source, norm_gain)).reshape(
            peers, slots, width
        )

    def double(codes, source, other):
        stacked = jnp.concatenate([source[:, :width], other[:, :width]], axis=0)
        return jnp.dot(spread(codes, 2), normalise(stacked, norm_gain)).reshape(
            peers, 2 * slots, width
        )

    def down_block(which_core, which_side, i=None):
        first, count = (0, local) if i is None else (i, 1)
        return lax.dynamic_slice(
            down_proj,
            (which_core * local + first, 0, 0, which_side * half),
            (count, 1, part, half),
        )[:, 0]

    first, second = activations[0], activations[1]

    own_codes = codes_of(expert_ids)
    outgoing, ids_sent = tie(single(own_codes[1], second), expert_ids)
    second_own = send(outgoing)
    side_ids = side_swap(ids_sent)
    first_side = side_swap(first)
    first_far = far_swap(first)
    far_ids = far_swap(jnp.stack([expert_ids, side_ids]))
    down_side = [side_swap(down_block(core, 1 - side, 0))]
    side_codes = codes_of(side_ids)
    outgoing = double(both_planes(own_codes[0], side_codes[0]), first, first_side)
    block, piece = (1, part, half), (1, part, half // 2)
    gate_up_send, side_next, *cross_next, core_blocks = cut(
        place,
        (gate_proj, up_proj, down_proj),
        [
            ((0, 1), True, 0, False, 0, (2 * local, part, width)),
            ((2,), False, 1, True, 0, block),
            ((2,), True, 0, True, 0, piece),
            ((2,), True, 0, True, half // 2, piece),
            ((2,), True, 1, True, 0, piece),
            ((2,), True, 1, True, half // 2, piece),
            ((2,), True, 0, False, 0, (local, part, half)),
        ],
    )
    column = router_weight.reshape(1, width)
    column_got = core_swap(column)
    pair = jnp.where(
        core == 0,
        jnp.concatenate([column, column_got]),
        jnp.concatenate([column_got, column]),
    )
    outgoing, second_own, first_far, far_ids, down_side[0], side_next, second, sent = tie(
        outgoing, second_own, first_far, far_ids, down_side[0], side_next, second,
        (gate_up_send, cross_next, core_blocks, pair),
    )
    gate_up_send, cross_next, core_blocks, pair = sent

    first_own = send(outgoing)
    first_far_side = side_swap(first_far)
    second_far = far_swap(second)
    down_side.append(side_swap(side_next))
    gate_up_got = core_swap(gate_up_send)
    down_cross = [cross_swap(cross_next[0])]
    pair_got = side_swap(pair)
    far_codes = codes_of(far_ids[0])
    far_side_codes = codes_of(far_ids[1])
    outgoing = double(both_planes(far_codes[0], far_side_codes[0]), first_far, first_far_side)
    all_own = [both_planes(own_codes[step], side_codes[step]) for step in range(steps)]
    all_far = [both_planes(far_codes[step], far_side_codes[step]) for step in range(steps)]
    gathers = (
        gather(all_own[0], 2, 0),
        gather(all_far[0], 2, 1),
        gather(all_own[1], 1, 0),
        gather(all_far[1], 1, 0),
    )
    outgoing, first_own, second_far, down_side[1], down_cross, gate_up_got, pair_got, cross_next = tie(
        outgoing, first_own, second_far, down_side[1], down_cross, gate_up_got, pair_got, cross_next
    )
    gathers, outgoing = tie(gathers, outgoing)

    first_relay = send(outgoing)
    second_far_side = side_swap(second_far)
    down_cross += [cross_swap(cross_next[1]), cross_swap(cross_next[2])]
    router = jnp.where(side == core, pair, pair_got)
    router = jnp.broadcast_to(router[:, None], (local, 16, width))
    outgoing = double(both_planes(far_codes[1], far_side_codes[1]), second_far, second_far_side)

    def start_experts(inputs, stride):
        return make_hidden(
            place,
            [each.reshape(-1, width) for each in inputs],
            router,
            gate_proj,
            up_proj,
            gate_up_got,
            capacity,
            stride,
        )

    def finish_experts(hidden, score, other):
        return make_result(
            place, hidden, other, score, down_proj, down_core, down_side, down_cross, capacity
        )

    def by_peer(result):
        return result.reshape(peers, 2 * slots, half + lanes)

    own_hidden, own_score, own_flipped = start_experts([first_own], slots)

    outgoing, first_relay, down_cross, cross_next, core_blocks, own_hidden, own_flipped, router = tie(
        outgoing, first_relay, down_cross, cross_next, core_blocks, own_hidden, own_flipped, router
    )

    second_relay = send(outgoing)
    down_cross.append(cross_swap(cross_next[3]))
    down_core = core_swap(core_blocks)
    own_other = side_swap(own_flipped)
    relay_hidden, relay_score, flipped = start_experts([first_relay], slots)
    relay_other = side_swap(flipped)
    own_result = by_peer(finish_experts(own_hidden, own_score, own_other))
    own_result, second_own = tie(own_result, second_own)
    low, high = peers // 4, peers * 5 // 8
    pieces = [side_swap(second_own[:low])]
    relay_result = by_peer(finish_experts(relay_hidden, relay_score, relay_other))
    outgoing = jnp.concatenate([own_result, relay_result], axis=1)
    outgoing, second_relay, second_own, pieces[0] = tie(
        outgoing, second_relay, second_own, pieces[0]
    )

    first_back = send(outgoing)
    pieces.append(side_swap(second_own[low:high]))
    relay_hidden, relay_score, flipped = start_experts([second_relay], slots)
    flipped, pieces[1] = tie(flipped, pieces[1])
    relay_other = side_swap(flipped)
    relay_other, second_own = tie(relay_other, second_own)
    pieces.append(side_swap(second_own[high:]))
    outgoing = by_peer(finish_experts(relay_hidden, relay_score, relay_other))
    outgoing, first_back, pieces = tie(outgoing, first_back, pieces)
    first_own_gather, first_far_gather, second_own_gather, second_far_gather = gathers

    def add(matrix, returned):
        return jnp.dot(
            matrix, returned.reshape(-1, half + lanes), preferred_element_type=jnp.float32
        )

    def finish(near, received):
        received = received.astype(jnp.float32)
        total = near[:, half : half + 1] + received[:, half : half + 1]
        mixture = ((near[:, :half] + received[:, :half]) / total).astype(jnp.bfloat16)
        return mixture[:rows], side_swap(mixture[rows:])

    def lay_out(own, received):
        low = jnp.where(side == 0, own, received)
        high = jnp.where(side == 0, received, own)
        return jnp.concatenate([low, high], axis=1)

    second_relay_back = send(outgoing)
    first_received = far_swap(add(first_far_gather, first_back).astype(jnp.bfloat16))
    own_hidden, own_score, flipped = start_experts([second_own, *pieces], peers * slots)
    result = finish_experts(own_hidden, own_score, side_swap(flipped))
    outgoing = by_peer(jnp.swapaxes(result.reshape(2, peers, slots, -1), 0, 1))
    first_near = add(first_own_gather, first_back)
    outgoing, second_relay_back, first_near = tie(outgoing, second_relay_back, first_near)

    second_own_back = send(outgoing)
    second_sums = add(second_far_gather, second_relay_back).astype(jnp.bfloat16)
    second_sums, first_received = tie(second_sums, first_received)
    second_received = far_swap(second_sums)
    first_out = finish(first_near, first_received)
    second_own_back, first_out = tie(second_own_back, first_out)
    second_out = finish(add(second_own_gather, second_own_back), second_received)
    return jnp.stack([lay_out(*first_out), lay_out(*second_out)])


def solution(mesh):
    sections, columns = mesh.shape["section"], mesh.shape["expert"]
    split = Mesh(
        mesh.devices.reshape(2, sections // 2, 2, columns // 2),
        ("side", "core", "far", "inner"),
    )
    weights = P(None, ("far", "inner"), ("side", "core"), None)
    return jax.shard_map(
        on_device,
        mesh=split,
        in_specs=(
            P(None, everywhere, None),
            P(),
            P(None, everywhere),
            weights,
            weights,
            weights,
            P(None, everywhere, None),
        ),
        out_specs=P(None, everywhere, None),
        check_vma=False,
    )
```

```python
import functools

import jax
import jax.numpy as jnp
from jax import lax
from jax.experimental import pallas as pl
from jax.experimental.pallas import tpu as pltpu
from jax.sharding import Mesh, PartitionSpec as P

epsilon = 1e-05
contract = (((1,), (1,)), ((), ()))
swap = [(0, 1), (1, 0)]
group = ("core", "inner")
everywhere = ("side", "core", "far", "inner")
vmem_bytes = 48 * 2**20
lanes = 128
block_rows = 128


def side_swap(values):
    return lax.ppermute(values, "side", swap)


def core_swap(values):
    return lax.ppermute(values, "core", swap)


def far_swap(values):
    return lax.ppermute(values, "far", swap)


def cross_swap(values):
    return lax.ppermute(values, ("side", "core"), [(0, 3), (1, 2), (2, 1), (3, 0)])


def send(values):
    return lax.all_to_all(values, group, split_axis=0, concat_axis=0, tiled=True)


def tie(*values):
    return lax.optimization_barrier(values)


def normalise(rows, norm_gain):
    current = rows.astype(jnp.float32)
    inverse_rms = lax.rsqrt(jnp.mean(current * current, axis=-1, keepdims=True) + epsilon)
    return (current * inverse_rms * norm_gain).astype(jnp.bfloat16)


def cut_kernel(plan, place, *refs):
    sources, outputs = refs[:3], refs[3 : 3 + len(plan)]
    kept, (sems, out_sems) = refs[3 + len(plan) : -2], refs[-2:]
    copies = []
    for n, blocks in enumerate(plan):
        height, column = 0, 0
        for which, other_core, first, count, other_side, offset, columns in blocks:
            source = sources[which]
            core = 1 - place[0] if other_core else place[0]
            side = 1 - place[1] if other_side else place[1]
            experts = pl.ds(core * (source.shape[0] // 2) + first, count)
            if columns < source.shape[3]:
                start = pl.multiple_of(side * (source.shape[3] // 2) + offset, lanes)
                block = source.at[experts, 0, :, pl.ds(start, columns)]
            else:
                block = source.at[experts, 0]
            spot = (pl.ds(height, count), slice(None), pl.ds(column, columns))
            if columns < source.shape[3]:
                column += columns
            else:
                height += count
            inner, outer = kept[n].at[spot], outputs[n].at[spot]
            copies.append(
                (
                    pltpu.make_async_copy(block, inner, sems.at[len(copies)]),
                    pltpu.make_async_copy(inner, outer, out_sems.at[len(copies)]),
                )
            )
    for inward, outward in copies:
        inward.start()
    for inward, outward in copies:
        inward.wait()
        outward.start()
    for inward, outward in copies:
        outward.wait()


def cut(place, weights, plan):
    anywhere = pl.BlockSpec(memory_space=pl.ANY)
    part, width = weights[0].shape[2:]
    shapes = []
    for blocks in plan:
        whole = blocks[0][6] == width
        height = sum(each[3] for each in blocks) if whole else blocks[0][3]
        columns = width if whole else sum(each[6] for each in blocks)
        shapes.append(jax.ShapeDtypeStruct((height, part, columns), jnp.bfloat16))
    total = sum(len(each) for each in plan)
    return pl.pallas_call(
        functools.partial(cut_kernel, plan),
        in_specs=[pl.BlockSpec(memory_space=pltpu.SMEM)] + [anywhere] * 3,
        out_specs=[anywhere] * len(plan),
        out_shape=shapes,
        scratch_shapes=[pltpu.VMEM(each.shape, each.dtype) for each in shapes]
        + [pltpu.SemaphoreType.DMA((total,))] * 2,
        compiler_params=pltpu.CompilerParams(vmem_limit_bytes=vmem_bytes),
        cost_estimate=pl.CostEstimate(flops=1, bytes_accessed=1, transcendentals=0),
    )(place, *weights)


def hidden_kernel(count, local, capacity, stride, place, *refs):
    inputs, (router, gate_proj, up_proj, got) = refs[:count], refs[count : count + 4]
    outputs, scratch = refs[count + 4 : -5], refs[-5:]
    hidden, score = outputs[:2]
    rows_kept, router_kept, weights, row_sems, weight_sems = scratch
    copies = [pltpu.make_async_copy(router, router_kept, row_sems.at[0])]
    first_row = 0
    for each in inputs:
        height = min(block_rows, each.shape[0])
        for start in range(0, each.shape[0], height):
            source, kept = each.at[pl.ds(start, height)], rows_kept.at[pl.ds(first_row, height)]
            copies.append(pltpu.make_async_copy(source, kept, row_sems.at[len(copies)]))
            first_row += height
    blocks = []
    for j in range(2):
        for i in range(local):
            if j == 0:
                sources = [ref.at[place[0] * local + i, 0] for ref in (gate_proj, up_proj)]
            else:
                sources = [got.at[i], got.at[local + i]]
            for n, source in enumerate(sources):
                blocks.append(
                    pltpu.make_async_copy(
                        source, weights.at[j, i, n], weight_sems.at[(j * local + i) * 2 + n]
                    )
                )
    for copy in copies + blocks[:2]:
        copy.start()
    for copy in copies:
        copy.wait()
    for copy in blocks[2:4]:
        copy.start()
    rows = rows_kept[...]
    owner = lax.broadcasted_iota(jnp.int32, (rows.shape[0], 1), 0) // capacity % local

    def product(matrix):
        return lax.dot_general(rows, matrix, contract, preferred_element_type=jnp.float32)

    gated = jnp.zeros((rows.shape[0], 1), jnp.float32)
    for i in range(local):
        logits = product(router_kept[i])
        gated = jnp.where(owner == i, 1.0 / (1.0 + jnp.exp(-logits[:, :1])), gated)
    score[...] = jnp.broadcast_to(gated, score.shape).astype(jnp.bfloat16)
    for j in range(2):
        chosen = None
        for i in range(local):
            for n in range(2):
                now = (j * local + i) * 2 + n
                blocks[now].wait()
                if now + 4 < len(blocks):
                    blocks[now + 4].start()
            gate_part = product(weights[j, i, 0])
            up_part = product(weights[j, i, 1])
            units = gate_part / (1.0 + jnp.exp(-gate_part)) * up_part
            chosen = units if i == 0 else jnp.where(owner == i, units, chosen)
        chosen = chosen.astype(jnp.bfloat16)
        hidden[j] = chosen
        for block in range(rows.shape[0] // stride if len(outputs) == 3 else 0):
            turned = pl.ds((block ^ 1) * stride, stride)
            outputs[2][j, turned, :] = chosen[block * stride : (block + 1) * stride]


def make_hidden(place, inputs, router, gate_proj, up_proj, got, capacity, stride):
    local, part, width = router.shape[0], *got.shape[1:]
    count = len(inputs)
    rows = sum(each.shape[0] for each in inputs)
    anywhere = pl.BlockSpec(memory_space=pl.ANY)
    near = pl.BlockSpec(memory_space=pltpu.VMEM)
    units = jax.ShapeDtypeStruct((2, rows, part), jnp.bfloat16)
    inside = stride % 16 == 0
    hidden, score, *flipped = pl.pallas_call(
        functools.partial(hidden_kernel, count, local, capacity, stride),
        in_specs=[pl.BlockSpec(memory_space=pltpu.SMEM)] + [anywhere] * (count + 4),
        out_specs=[near] * (3 if inside else 2),
        out_shape=[units, jax.ShapeDtypeStruct((rows, lanes), jnp.bfloat16)] + [units] * inside,
        scratch_shapes=[
            pltpu.VMEM((rows, width), jnp.bfloat16),
            pltpu.VMEM(router.shape, jnp.bfloat16),
            pltpu.VMEM((2, local, 2, part, width), jnp.bfloat16),
            pltpu.SemaphoreType.DMA((rows // min(16, rows) + 1,)),
            pltpu.SemaphoreType.DMA((4 * local,)),
        ],
        compiler_params=pltpu.CompilerParams(vmem_limit_bytes=vmem_bytes),
        cost_estimate=pl.CostEstimate(flops=1, bytes_accessed=1, transcendentals=0),
    )(place, *inputs, router, gate_proj, up_proj, got)
    if not inside:
        flipped = [jnp.flip(hidden.reshape(2, -1, 2, stride, part), axis=2).reshape(hidden.shape)]
    return hidden, score, flipped[0]


def result_kernel(local, capacity, plan, place, hidden, other, score, down_proj, down_core, *refs):
    got, (result, weights, sems) = refs[:-3], refs[-3:]
    part, half = down_core.shape[1:]
    blocks = [[] for _ in range(4 * local)]

    def add_copy(block, source, spot):
        sem = sems.at[sum(len(each) for each in blocks)]
        blocks[block].append(pltpu.make_async_copy(source, spot, sem))

    for i in range(local):
        columns = pl.ds(pl.multiple_of(place[1] * half, lanes), half)
        add_copy(4 * i, down_proj.at[place[0] * local + i, 0, :, columns], weights.at[i, 0])
        add_copy(4 * i + 1, down_core.at[i], weights.at[i, 1])
        for which, column, expert, cross, first, count in plan:
            if expert == i:
                source = got[which].at[0, :, pl.ds(column, count)]
                add_copy(4 * i + 2 + cross, source, weights.at[i, 2 + cross, :, pl.ds(first, count)])
    for block in blocks:
        for copy in block:
            copy.start()
    rows = hidden.shape[1]
    owner = lax.broadcasted_iota(jnp.int32, (rows, 1), 0) // capacity % local
    units = [hidden[0], hidden[1], other[0], other[1]]
    total = None
    for i in range(local):
        for n in range(4):
            for copy in blocks[i * 4 + n]:
                copy.wait()
            mine = jnp.where(owner == i, units[n], jnp.zeros_like(units[n]))
            term = jnp.dot(mine, weights[i, n], preferred_element_type=jnp.float32)
            total = term if total is None else total + term
    gated = total * score[:, :1].astype(jnp.float32)
    result[:, :half] = gated.astype(jnp.bfloat16)
    result[:, half:] = score[...]


def make_result(place, hidden, other, score, down_proj, down_core, got, plan, capacity):
    local, part, half = down_core.shape
    rows = hidden.shape[1]
    anywhere = pl.BlockSpec(memory_space=pl.ANY)
    near = pl.BlockSpec(memory_space=pltpu.VMEM)
    return pl.pallas_call(
        functools.partial(result_kernel, local, capacity, plan),
        in_specs=[pl.BlockSpec(memory_space=pltpu.SMEM)] + [near] * 3 + [anywhere] * (2 + len(got)),
        out_specs=near,
        out_shape=jax.ShapeDtypeStruct((rows, half + lanes), jnp.bfloat16),
        scratch_shapes=[
            pltpu.VMEM((local, 4, part, half), jnp.bfloat16),
            pltpu.SemaphoreType.DMA((2 * local + len(plan),)),
        ],
        compiler_params=pltpu.CompilerParams(vmem_limit_bytes=vmem_bytes),
        cost_estimate=pl.CostEstimate(flops=1, bytes_accessed=1, transcendentals=0),
    )(place, hidden, other, score, down_proj, down_core, *got)


def on_device(activations, norm_gain, router_weight, gate_proj, up_proj, down_proj, expert_ids):
    steps, rows, width = activations.shape
    top = expert_ids.shape[2]
    cores, fars, inners = (lax.axis_size(name) for name in ("core", "far", "inner"))
    local = gate_proj.shape[0] // cores
    experts = gate_proj.shape[0] * fars * inners
    capacity = max(2, 2 * top * rows // experts)
    part = gate_proj.shape[2]
    half = width // 2
    side, core, far = (lax.axis_index(name) for name in ("side", "core", "far"))
    place = jnp.stack([core, side]).astype(jnp.int32)
    peers = cores * inners
    slots = local * capacity
    places = experts * capacity

    def codes_of(ids):
        flat = ids.reshape(steps, 1, 1, -1)
        before = jnp.arange(rows * top, dtype=jnp.int32) // top < jnp.arange(
            rows, dtype=jnp.int32
        ).reshape(rows, 1, 1)
        earlier = jnp.sum(((ids[..., None] == flat) & before).astype(jnp.int32), axis=3)
        return ids * capacity + earlier

    def spots(kinds, kind, planes):
        shape = (cores, inners, kinds, planes, local, capacity)
        c, n, k, q, l, t = (lax.broadcasted_iota(jnp.int32, shape, axis) for axis in range(6))
        spot = ((((c * local + l) * fars + far) * inners + n) * capacity + t) + q * places
        return jnp.where(k == kind, spot, -1).reshape(-1)

    def both_planes(near, other):
        return jnp.concatenate([near, other + places], axis=0)

    def matching(left, right):
        return jnp.any(left == right, axis=0).astype(jnp.bfloat16)

    def spread(codes, planes):
        spot = spots(1, 0, planes)
        return matching(spot[None, :, None], codes.T[:, None, :])

    def gather(codes, kinds, kind):
        spot = spots(kinds, kind, 2)
        return matching(codes.T[:, :, None], spot[None, None, :])

    def single(codes, source):
        return jnp.dot(spread(codes, 1), normalise(source, norm_gain)).reshape(
            peers, slots, width
        )

    def double(codes, source, other):
        stacked = jnp.concatenate([source[:, :width], other[:, :width]], axis=0)
        return jnp.dot(spread(codes, 2), normalise(stacked, norm_gain)).reshape(
            peers, 2 * slots, width
        )

    first, second = activations[0], activations[1]

    own_codes = codes_of(expert_ids)
    outgoing, ids_sent = tie(single(own_codes[1], second), expert_ids)
    second_own = send(outgoing)
    side_ids = side_swap(ids_sent)
    first_side = side_swap(first)
    first_far = far_swap(first)
    far_ids = far_swap(jnp.stack([expert_ids, side_ids]))
    weights = (gate_proj, up_proj, down_proj)
    unit = half // 4

    def of_down(cross, i, first, count):
        return (2, bool(cross), i, 1, True, first * unit, count * unit)

    sent_units = (
        ((0, 0, 0, 4), (0, 1, 0, 1)),
        ((0, 1, 1, 3),),
        ((1, 0, 0, 2),),
        ((1, 0, 2, 2), (1, 1, 0, 2)),
        ((1, 1, 2, 2),),
    )
    pieces_of = [[of_down(*each) for each in piece] for piece in sent_units]
    result_plan = []
    for which, piece in enumerate(sent_units):
        column = 0
        for cross, i, start, count in piece:
            result_plan.append((which, column, i, cross, start * unit, count * unit))
            column += count * unit
    result_plan = tuple(result_plan)
    down_got = [side_swap(cut(place, weights, [pieces_of[0]])[0])]
    side_codes = codes_of(side_ids)
    outgoing = double(both_planes(own_codes[0], side_codes[0]), first, first_side)
    gate_up_send, core_blocks, *to_send = cut(
        place,
        weights,
        [
            [(which, True, 0, local, False, 0, width) for which in (0, 1)],
            [(2, True, 0, local, False, 0, half)],
            *pieces_of[1:],
        ],
    )
    column = router_weight.reshape(1, width)
    column_got = core_swap(column)
    pair = jnp.where(
        core == 0,
        jnp.concatenate([column, column_got]),
        jnp.concatenate([column_got, column]),
    )
    outgoing, second_own, first_far, far_ids, down_got, second, sent = tie(
        outgoing, second_own, first_far, far_ids, down_got, second,
        (gate_up_send, to_send, core_blocks, pair),
    )
    gate_up_send, to_send, core_blocks, pair = sent

    first_own = send(outgoing)
    first_far_side = side_swap(first_far)
    second_far = far_swap(second)
    down_got += [side_swap(to_send[0]), cross_swap(to_send[1])]
    gate_up_got = core_swap(gate_up_send)
    pair_got = side_swap(pair)
    far_codes = codes_of(far_ids[0])
    far_side_codes = codes_of(far_ids[1])
    outgoing = double(both_planes(far_codes[0], far_side_codes[0]), first_far, first_far_side)
    all_own = [both_planes(own_codes[step], side_codes[step]) for step in range(steps)]
    all_far = [both_planes(far_codes[step], far_side_codes[step]) for step in range(steps)]
    gathers = (
        gather(all_own[0], 2, 0),
        gather(all_far[0], 2, 1),
        gather(all_own[1], 1, 0),
        gather(all_far[1], 1, 0),
    )
    outgoing, first_own, second_far, down_got, gate_up_got, pair_got, to_send = tie(
        outgoing, first_own, second_far, down_got, gate_up_got, pair_got, to_send
    )
    gathers, outgoing = tie(gathers, outgoing)

    first_relay = send(outgoing)
    second_far_side = side_swap(second_far)
    down_got.append(cross_swap(to_send[2]))
    router = jnp.where(side == core, pair, pair_got)
    router = jnp.broadcast_to(router[:, None], (local, 16, width))
    outgoing = double(both_planes(far_codes[1], far_side_codes[1]), second_far, second_far_side)

    def start_experts(inputs, stride):
        return make_hidden(
            place,
            [each.reshape(-1, width) for each in inputs],
            router,
            gate_proj,
            up_proj,
            gate_up_got,
            capacity,
            stride,
        )

    def finish_experts(hidden, score, other):
        return make_result(
            place, hidden, other, score, down_proj, down_core, down_got, result_plan, capacity
        )

    def by_peer(result):
        return result.reshape(peers, 2 * slots, half + lanes)

    own_hidden, own_score, own_flipped = start_experts([first_own], slots)

    outgoing, first_relay, down_got, to_send, core_blocks, own_hidden, own_flipped, router = tie(
        outgoing, first_relay, down_got, to_send, core_blocks, own_hidden, own_flipped, router
    )

    second_relay = send(outgoing)
    down_got.append(cross_swap(to_send[3]))
    down_core = core_swap(core_blocks)
    own_other = side_swap(own_flipped)
    relay_hidden, relay_score, flipped = start_experts([first_relay], slots)
    relay_other = side_swap(flipped)
    own_result = by_peer(finish_experts(own_hidden, own_score, own_other))
    own_result, second_own = tie(own_result, second_own)
    low, high = peers // 4, peers * 5 // 8
    pieces = [side_swap(second_own[:low])]
    relay_result = by_peer(finish_experts(relay_hidden, relay_score, relay_other))
    outgoing = jnp.concatenate([own_result, relay_result], axis=1)
    outgoing, second_relay, second_own, pieces[0] = tie(
        outgoing, second_relay, second_own, pieces[0]
    )

    first_back = send(outgoing)
    pieces.append(side_swap(second_own[low:high]))
    relay_hidden, relay_score, flipped = start_experts([second_relay], slots)
    flipped, pieces[1] = tie(flipped, pieces[1])
    relay_other = side_swap(flipped)
    relay_other, second_own = tie(relay_other, second_own)
    pieces.append(side_swap(second_own[high:]))
    outgoing = by_peer(finish_experts(relay_hidden, relay_score, relay_other))
    outgoing, first_back, pieces = tie(outgoing, first_back, pieces)
    first_own_gather, first_far_gather, second_own_gather, second_far_gather = gathers

    def add(matrix, returned):
        return jnp.dot(
            matrix, returned.reshape(-1, half + lanes), preferred_element_type=jnp.float32
        )

    def finish(near, received):
        total = near[:, half : half + 1] + received[:, half : half + 1].astype(jnp.float32)
        sums = near[:, :half] + received[:, :half].astype(jnp.float32)
        mixture = (sums / total).astype(jnp.bfloat16)
        return mixture[:rows], side_swap(mixture[rows:])

    def lay_out(own, received):
        low = jnp.where(side == 0, own, received)
        high = jnp.where(side == 0, received, own)
        return jnp.concatenate([low, high], axis=1)

    second_relay_back = send(outgoing)
    first_received = far_swap(add(first_far_gather, first_back).astype(jnp.bfloat16))
    own_hidden, own_score, flipped = start_experts([second_own, *pieces], peers * slots)
    result = finish_experts(own_hidden, own_score, side_swap(flipped))
    outgoing = by_peer(jnp.swapaxes(result.reshape(2, peers, slots, -1), 0, 1))
    first_near = add(first_own_gather, first_back)
    outgoing, second_relay_back, first_near = tie(outgoing, second_relay_back, first_near)

    second_own_back = send(outgoing)
    second_sums = add(second_far_gather, second_relay_back).astype(jnp.bfloat16)
    second_received = far_swap(second_sums)
    first_out = finish(first_near, first_received)
    second_own_back, first_out = tie(second_own_back, first_out)
    second_out = finish(add(second_own_gather, second_own_back), second_received)
    return jnp.stack([lay_out(*first_out), lay_out(*second_out)])


def solution(mesh):
    sections, columns = mesh.shape["section"], mesh.shape["expert"]
    split = Mesh(
        mesh.devices.reshape(2, sections // 2, 2, columns // 2),
        ("side", "core", "far", "inner"),
    )
    weights = P(None, ("far", "inner"), ("side", "core"), None)
    return jax.shard_map(
        on_device,
        mesh=split,
        in_specs=(
            P(None, everywhere, None),
            P(),
            P(None, everywhere),
            weights,
            weights,
            weights,
            P(None, everywhere, None),
        ),
        out_specs=P(None, everywhere, None),
        check_vma=False,
    )
```

```python
import functools

import jax
import jax.numpy as jnp
from jax import lax
from jax.experimental import pallas as pl
from jax.experimental.pallas import tpu as pltpu
from jax.sharding import Mesh, PartitionSpec as P

epsilon = 1e-05
contract = (((1,), (1,)), ((), ()))
swap = [(0, 1), (1, 0)]
group = ("core", "inner")
everywhere = ("side", "core", "far", "inner")
vmem_bytes = 48 * 2**20
lanes = 128
block_rows = 128


def side_swap(values):
    return lax.ppermute(values, "side", swap)


def core_swap(values):
    return lax.ppermute(values, "core", swap)


def far_swap(values):
    return lax.ppermute(values, "far", swap)


def cross_swap(values):
    return lax.ppermute(values, ("side", "core"), [(0, 3), (1, 2), (2, 1), (3, 0)])


def send(values):
    return lax.all_to_all(values, group, split_axis=0, concat_axis=0, tiled=True)


def tie(*values):
    return lax.optimization_barrier(values)


def normalise(rows, norm_gain):
    current = rows.astype(jnp.float32)
    inverse_rms = lax.rsqrt(jnp.mean(current * current, axis=-1, keepdims=True) + epsilon)
    return (current * inverse_rms * norm_gain).astype(jnp.bfloat16)


def cut_kernel(plan, place, *refs):
    sources, outputs = refs[:3], refs[3 : 3 + len(plan)]
    kept, (sems, out_sems) = refs[3 + len(plan) : -2], refs[-2:]
    copies = []
    for n, blocks in enumerate(plan):
        height, column = 0, 0
        for which, other_core, first, count, other_side, offset, columns in blocks:
            source = sources[which]
            core = 1 - place[0] if other_core else place[0]
            side = 1 - place[1] if other_side else place[1]
            experts = pl.ds(core * (source.shape[0] // 2) + first, count)
            if columns < source.shape[3]:
                start = pl.multiple_of(side * (source.shape[3] // 2) + offset, lanes)
                block = source.at[experts, 0, :, pl.ds(start, columns)]
            else:
                block = source.at[experts, 0]
            spot = (pl.ds(height, count), slice(None), pl.ds(column, columns))
            if columns < source.shape[3]:
                column += columns
            else:
                height += count
            inner, outer = kept[n].at[spot], outputs[n].at[spot]
            copies.append(
                (
                    pltpu.make_async_copy(block, inner, sems.at[len(copies)]),
                    pltpu.make_async_copy(inner, outer, out_sems.at[len(copies)]),
                )
            )
    for inward, outward in copies:
        inward.start()
    for inward, outward in copies:
        inward.wait()
        outward.start()
    for inward, outward in copies:
        outward.wait()


def cut(place, weights, plan):
    anywhere = pl.BlockSpec(memory_space=pl.ANY)
    part, width = weights[0].shape[2:]
    shapes = []
    for blocks in plan:
        whole = blocks[0][6] == width
        height = sum(each[3] for each in blocks) if whole else blocks[0][3]
        columns = width if whole else sum(each[6] for each in blocks)
        shapes.append(jax.ShapeDtypeStruct((height, part, columns), jnp.bfloat16))
    total = sum(len(each) for each in plan)
    return pl.pallas_call(
        functools.partial(cut_kernel, plan),
        in_specs=[pl.BlockSpec(memory_space=pltpu.SMEM)] + [anywhere] * 3,
        out_specs=[anywhere] * len(plan),
        out_shape=shapes,
        scratch_shapes=[pltpu.VMEM(each.shape, each.dtype) for each in shapes]
        + [pltpu.SemaphoreType.DMA((total,))] * 2,
        compiler_params=pltpu.CompilerParams(vmem_limit_bytes=vmem_bytes),
        cost_estimate=pl.CostEstimate(flops=1, bytes_accessed=1, transcendentals=0),
    )(place, *weights)


def hidden_kernel(count, local, capacity, stride, place, *refs):
    inputs, (router, gate_proj, up_proj, got) = refs[:count], refs[count : count + 4]
    outputs, scratch = refs[count + 4 : -5], refs[-5:]
    hidden, score = outputs[:2]
    rows_kept, router_kept, weights, row_sems, weight_sems = scratch
    copies = [pltpu.make_async_copy(router, router_kept, row_sems.at[0])]
    first_row = 0
    for each in inputs:
        height = min(block_rows, each.shape[0])
        for start in range(0, each.shape[0], height):
            source, kept = each.at[pl.ds(start, height)], rows_kept.at[pl.ds(first_row, height)]
            copies.append(pltpu.make_async_copy(source, kept, row_sems.at[len(copies)]))
            first_row += height
    blocks = []
    for j in range(2):
        for i in range(local):
            if j == 0:
                sources = [ref.at[place[0] * local + i, 0] for ref in (gate_proj, up_proj)]
            else:
                sources = [got.at[i], got.at[local + i]]
            for n, source in enumerate(sources):
                blocks.append(
                    pltpu.make_async_copy(
                        source, weights.at[j, i, n], weight_sems.at[(j * local + i) * 2 + n]
                    )
                )
    for copy in copies + blocks[:2]:
        copy.start()
    for copy in copies:
        copy.wait()
    for copy in blocks[2:4]:
        copy.start()
    rows = rows_kept[...]
    owner = lax.broadcasted_iota(jnp.int32, (rows.shape[0], 1), 0) // capacity % local

    def product(matrix):
        return lax.dot_general(rows, matrix, contract, preferred_element_type=jnp.float32)

    gated = jnp.zeros((rows.shape[0], 1), jnp.float32)
    copies_of = router_kept.shape[1]
    logits = product(router_kept[...].reshape(local * copies_of, router_kept.shape[2]))
    for i in range(local):
        column = logits[:, i * copies_of : i * copies_of + 1]
        gated = jnp.where(owner == i, 1.0 / (1.0 + jnp.exp(-column)), gated)
    score[...] = jnp.broadcast_to(gated, score.shape).astype(jnp.bfloat16)
    for j in range(2):
        chosen = None
        for i in range(local):
            for n in range(2):
                now = (j * local + i) * 2 + n
                blocks[now].wait()
                if now + 4 < len(blocks):
                    blocks[now + 4].start()
            gate_part = product(weights[j, i, 0])
            up_part = product(weights[j, i, 1])
            units = gate_part / (1.0 + jnp.exp(-gate_part)) * up_part
            chosen = units if i == 0 else jnp.where(owner == i, units, chosen)
        chosen = chosen.astype(jnp.bfloat16)
        hidden[j] = chosen
        for block in range(rows.shape[0] // stride if len(outputs) == 3 else 0):
            turned = pl.ds((block ^ 1) * stride, stride)
            outputs[2][j, turned, :] = chosen[block * stride : (block + 1) * stride]


def make_hidden(place, inputs, router, gate_proj, up_proj, got, capacity, stride):
    local, part, width = router.shape[0], *got.shape[1:]
    count = len(inputs)
    rows = sum(each.shape[0] for each in inputs)
    anywhere = pl.BlockSpec(memory_space=pl.ANY)
    near = pl.BlockSpec(memory_space=pltpu.VMEM)
    units = jax.ShapeDtypeStruct((2, rows, part), jnp.bfloat16)
    inside = stride % 16 == 0
    hidden, score, *flipped = pl.pallas_call(
        functools.partial(hidden_kernel, count, local, capacity, stride),
        in_specs=[pl.BlockSpec(memory_space=pltpu.SMEM)] + [anywhere] * (count + 4),
        out_specs=[near] * (3 if inside else 2),
        out_shape=[units, jax.ShapeDtypeStruct((rows, lanes), jnp.bfloat16)] + [units] * inside,
        scratch_shapes=[
            pltpu.VMEM((rows, width), jnp.bfloat16),
            pltpu.VMEM(router.shape, jnp.bfloat16),
            pltpu.VMEM((2, local, 2, part, width), jnp.bfloat16),
            pltpu.SemaphoreType.DMA((rows // min(16, rows) + 1,)),
            pltpu.SemaphoreType.DMA((4 * local,)),
        ],
        compiler_params=pltpu.CompilerParams(vmem_limit_bytes=vmem_bytes),
        cost_estimate=pl.CostEstimate(flops=1, bytes_accessed=1, transcendentals=0),
    )(place, *inputs, router, gate_proj, up_proj, got)
    if not inside:
        flipped = [jnp.flip(hidden.reshape(2, -1, 2, stride, part), axis=2).reshape(hidden.shape)]
    return hidden, score, flipped[0]


def result_kernel(local, capacity, plan, place, hidden, other, score, down_proj, down_core, *refs):
    got, (result, weights, sems) = refs[:-3], refs[-3:]
    part, half = down_core.shape[1:]
    blocks = [[] for _ in range(4 * local)]

    def add_copy(block, source, spot):
        sem = sems.at[sum(len(each) for each in blocks)]
        blocks[block].append(pltpu.make_async_copy(source, spot, sem))

    for i in range(local):
        columns = pl.ds(pl.multiple_of(place[1] * half, lanes), half)
        add_copy(4 * i, down_proj.at[place[0] * local + i, 0, :, columns], weights.at[i, 0])
        add_copy(4 * i + 1, down_core.at[i], weights.at[i, 1])
        for which, column, expert, cross, first, count in plan:
            if expert == i:
                source = got[which].at[0, :, pl.ds(column, count)]
                add_copy(4 * i + 2 + cross, source, weights.at[i, 2 + cross, :, pl.ds(first, count)])
    for block in blocks:
        for copy in block:
            copy.start()
    rows = hidden.shape[1]
    owner = lax.broadcasted_iota(jnp.int32, (rows, 1), 0) // capacity % local
    units = [hidden[0], hidden[1], other[0], other[1]]
    total = None
    for i in range(local):
        for n in range(4):
            for copy in blocks[i * 4 + n]:
                copy.wait()
            mine = jnp.where(owner == i, units[n], jnp.zeros_like(units[n]))
            term = jnp.dot(mine, weights[i, n], preferred_element_type=jnp.float32)
            total = term if total is None else total + term
    gated = total * score[:, :1].astype(jnp.float32)
    result[:, :half] = gated.astype(jnp.bfloat16)
    result[:, half:] = score[...]


def make_result(place, hidden, other, score, down_proj, down_core, got, plan, capacity):
    local, part, half = down_core.shape
    rows = hidden.shape[1]
    anywhere = pl.BlockSpec(memory_space=pl.ANY)
    near = pl.BlockSpec(memory_space=pltpu.VMEM)
    return pl.pallas_call(
        functools.partial(result_kernel, local, capacity, plan),
        in_specs=[pl.BlockSpec(memory_space=pltpu.SMEM)] + [near] * 3 + [anywhere] * (2 + len(got)),
        out_specs=near,
        out_shape=jax.ShapeDtypeStruct((rows, half + lanes), jnp.bfloat16),
        scratch_shapes=[
            pltpu.VMEM((local, 4, part, half), jnp.bfloat16),
            pltpu.SemaphoreType.DMA((2 * local + len(plan),)),
        ],
        compiler_params=pltpu.CompilerParams(vmem_limit_bytes=vmem_bytes),
        cost_estimate=pl.CostEstimate(flops=1, bytes_accessed=1, transcendentals=0),
    )(place, hidden, other, score, down_proj, down_core, *got)


def on_device(activations, norm_gain, router_weight, gate_proj, up_proj, down_proj, expert_ids):
    steps, rows, width = activations.shape
    top = expert_ids.shape[2]
    cores, fars, inners = (lax.axis_size(name) for name in ("core", "far", "inner"))
    local = gate_proj.shape[0] // cores
    experts = gate_proj.shape[0] * fars * inners
    capacity = max(2, 2 * top * rows // experts)
    part = gate_proj.shape[2]
    half = width // 2
    side, core, far = (lax.axis_index(name) for name in ("side", "core", "far"))
    place = jnp.stack([core, side]).astype(jnp.int32)
    peers = cores * inners
    slots = local * capacity
    places = experts * capacity

    def codes_of(ids):
        flat = ids.reshape(steps, 1, 1, -1)
        before = jnp.arange(rows * top, dtype=jnp.int32) // top < jnp.arange(
            rows, dtype=jnp.int32
        ).reshape(rows, 1, 1)
        earlier = jnp.sum(((ids[..., None] == flat) & before).astype(jnp.int32), axis=3)
        return ids * capacity + earlier

    def spots(kinds, kind, planes):
        shape = (cores, inners, kinds, planes, local, capacity)
        c, n, k, q, l, t = (lax.broadcasted_iota(jnp.int32, shape, axis) for axis in range(6))
        spot = ((((c * local + l) * fars + far) * inners + n) * capacity + t) + q * places
        return jnp.where(k == kind, spot, -1).reshape(-1)

    def both_planes(near, other):
        return jnp.concatenate([near, other + places], axis=0)

    def matching(left, right):
        return jnp.any(left == right, axis=0).astype(jnp.bfloat16)

    def spread(codes, planes):
        spot = spots(1, 0, planes)
        return matching(spot[None, :, None], codes.T[:, None, :])

    def gather(codes, kinds, kind):
        spot = spots(kinds, kind, 2)
        return matching(codes.T[:, :, None], spot[None, None, :])

    def single(codes, source):
        return jnp.dot(spread(codes, 1), normalise(source, norm_gain)).reshape(
            peers, slots, width
        )

    def double(codes, source, other):
        stacked = jnp.concatenate([source[:, :width], other[:, :width]], axis=0)
        return jnp.dot(spread(codes, 2), normalise(stacked, norm_gain)).reshape(
            peers, 2 * slots, width
        )

    first, second = activations[0], activations[1]

    own_codes = codes_of(expert_ids)
    outgoing, ids_sent = tie(single(own_codes[1], second), expert_ids)
    second_own = send(outgoing)
    side_ids = side_swap(ids_sent)
    first_side = side_swap(first)
    first_far = far_swap(first)
    far_ids = far_swap(jnp.stack([expert_ids, side_ids]))
    weights = (gate_proj, up_proj, down_proj)
    unit = half // 4

    def of_down(cross, i, first, count):
        return (2, bool(cross), i, 1, True, first * unit, count * unit)

    sent_units = (
        ((0, 0, 0, 4), (0, 1, 0, 1)),
        ((0, 1, 1, 3),),
        ((1, 0, 0, 2),),
        ((1, 0, 2, 2), (1, 1, 0, 2)),
        ((1, 1, 2, 2),),
    )
    pieces_of = [[of_down(*each) for each in piece] for piece in sent_units]
    result_plan = []
    for which, piece in enumerate(sent_units):
        column = 0
        for cross, i, start, count in piece:
            result_plan.append((which, column, i, cross, start * unit, count * unit))
            column += count * unit
    result_plan = tuple(result_plan)
    down_got = [side_swap(cut(place, weights, [pieces_of[0]])[0])]
    side_codes = codes_of(side_ids)
    outgoing = double(both_planes(own_codes[0], side_codes[0]), first, first_side)
    gate_up_send, core_blocks, *to_send = cut(
        place,
        weights,
        [
            [(which, True, 0, local, False, 0, width) for which in (0, 1)],
            [(2, True, 0, local, False, 0, half)],
            *pieces_of[1:],
        ],
    )
    column = router_weight.reshape(1, width)
    column_got = core_swap(column)
    pair = jnp.where(
        core == 0,
        jnp.concatenate([column, column_got]),
        jnp.concatenate([column_got, column]),
    )
    outgoing, second_own, first_far, far_ids, down_got, second, sent = tie(
        outgoing, second_own, first_far, far_ids, down_got, second,
        (gate_up_send, to_send, core_blocks, pair),
    )
    gate_up_send, to_send, core_blocks, pair = sent

    first_own = send(outgoing)
    first_far_side = side_swap(first_far)
    second_far = far_swap(second)
    down_got += [side_swap(to_send[0]), cross_swap(to_send[1])]
    gate_up_got = core_swap(gate_up_send)
    pair_got = side_swap(pair)
    far_codes = codes_of(far_ids[0])
    far_side_codes = codes_of(far_ids[1])
    outgoing = double(both_planes(far_codes[0], far_side_codes[0]), first_far, first_far_side)
    all_own = [both_planes(own_codes[step], side_codes[step]) for step in range(steps)]
    all_far = [both_planes(far_codes[step], far_side_codes[step]) for step in range(steps)]
    gathers = (
        gather(all_own[0], 2, 0),
        gather(all_far[0], 2, 1),
        gather(all_own[1], 1, 0),
        gather(all_far[1], 1, 0),
    )
    outgoing, first_own, second_far, down_got, gate_up_got, pair_got, to_send = tie(
        outgoing, first_own, second_far, down_got, gate_up_got, pair_got, to_send
    )
    gathers, outgoing = tie(gathers, outgoing)

    first_relay = send(outgoing)
    second_far_side = side_swap(second_far)
    down_got.append(cross_swap(to_send[2]))
    router = jnp.where(side == core, pair, pair_got)
    router = jnp.broadcast_to(router[:, None], (local, 16, width))
    outgoing = double(both_planes(far_codes[1], far_side_codes[1]), second_far, second_far_side)

    def start_experts(inputs, stride):
        return make_hidden(
            place,
            [each.reshape(-1, width) for each in inputs],
            router,
            gate_proj,
            up_proj,
            gate_up_got,
            capacity,
            stride,
        )

    def finish_experts(hidden, score, other):
        return make_result(
            place, hidden, other, score, down_proj, down_core, down_got, result_plan, capacity
        )

    def by_peer(result):
        return result.reshape(peers, 2 * slots, half + lanes)

    own_hidden, own_score, own_flipped = start_experts([first_own], slots)

    outgoing, first_relay, down_got, to_send, core_blocks, own_hidden, own_flipped, router = tie(
        outgoing, first_relay, down_got, to_send, core_blocks, own_hidden, own_flipped, router
    )

    second_relay = send(outgoing)
    down_got.append(cross_swap(to_send[3]))
    down_core = core_swap(core_blocks)
    own_other = side_swap(own_flipped)
    relay_hidden, relay_score, flipped = start_experts([first_relay], slots)
    relay_other = side_swap(flipped)
    own_result = by_peer(finish_experts(own_hidden, own_score, own_other))
    own_result, second_own = tie(own_result, second_own)
    low, high = peers // 4, peers * 5 // 8
    pieces = [side_swap(second_own[:low])]
    relay_result = by_peer(finish_experts(relay_hidden, relay_score, relay_other))
    outgoing = jnp.concatenate([own_result, relay_result], axis=1)
    outgoing, second_relay, second_own, pieces[0] = tie(
        outgoing, second_relay, second_own, pieces[0]
    )

    first_back = send(outgoing)
    pieces.append(side_swap(second_own[low:high]))
    relay_hidden, relay_score, flipped = start_experts([second_relay], slots)
    flipped, pieces[1] = tie(flipped, pieces[1])
    relay_other = side_swap(flipped)
    relay_other, second_own = tie(relay_other, second_own)
    pieces.append(side_swap(second_own[high:]))
    outgoing = by_peer(finish_experts(relay_hidden, relay_score, relay_other))
    outgoing, first_back, pieces = tie(outgoing, first_back, pieces)
    first_own_gather, first_far_gather, second_own_gather, second_far_gather = gathers

    def add(matrix, returned):
        return jnp.dot(
            matrix, returned.reshape(-1, half + lanes), preferred_element_type=jnp.float32
        )

    def finish(near, received):
        total = near[:, half : half + 1] + received[:, half : half + 1].astype(jnp.float32)
        sums = near[:, :half] + received[:, :half].astype(jnp.float32)
        mixture = (sums / total).astype(jnp.bfloat16)
        return mixture[:rows], side_swap(mixture[rows:])

    def lay_out(own, received):
        low = jnp.where(side == 0, own, received)
        high = jnp.where(side == 0, received, own)
        return jnp.concatenate([low, high], axis=1)

    second_relay_back = send(outgoing)
    first_received = far_swap(add(first_far_gather, first_back).astype(jnp.bfloat16))
    own_hidden, own_score, flipped = start_experts([second_own, *pieces], peers * slots)
    result = finish_experts(own_hidden, own_score, side_swap(flipped))
    outgoing = by_peer(jnp.swapaxes(result.reshape(2, peers, slots, -1), 0, 1))
    first_near = add(first_own_gather, first_back)
    outgoing, second_relay_back, first_near = tie(outgoing, second_relay_back, first_near)

    second_own_back = send(outgoing)
    second_sums = add(second_far_gather, second_relay_back).astype(jnp.bfloat16)
    second_received = far_swap(second_sums)
    first_out = finish(first_near, first_received)
    second_own_back, first_out = tie(second_own_back, first_out)
    second_out = finish(add(second_own_gather, second_own_back), second_received)
    return jnp.stack([lay_out(*first_out), lay_out(*second_out)])


def solution(mesh):
    sections, columns = mesh.shape["section"], mesh.shape["expert"]
    split = Mesh(
        mesh.devices.reshape(2, sections // 2, 2, columns // 2),
        ("side", "core", "far", "inner"),
    )
    weights = P(None, ("far", "inner"), ("side", "core"), None)
    return jax.shard_map(
        on_device,
        mesh=split,
        in_specs=(
            P(None, everywhere, None),
            P(),
            P(None, everywhere),
            weights,
            weights,
            weights,
            P(None, everywhere, None),
        ),
        out_specs=P(None, everywhere, None),
        check_vma=False,
    )
```
